32 devices in a mesh: groups: 2 (over x), wide: 16 (over z, y, core).
Axes of the slice: x: 2, y: 2, z: 4, core: 2. Of those that a mesh axis runs over, the one named last changes fastest.
Arguments:
- residual: bfloat16 [4096, 2048], P(('groups', 'wide')), parts along dimension 0, may hold values from -6 to 6
- queries: bfloat16 [4096, 2048], P(('groups', 'wide')), parts along dimension 0, may hold values from -160 to 160
- new_keys: bfloat16 [4096, 256], P(('groups', 'wide')), parts along dimension 0, may hold values from -6 to 6
- new_values: bfloat16 [4096, 256], P(('groups', 'wide')), parts along dimension 0, may hold values from -6 to 6
- cache_keys: bfloat16 [32, 2048, 256], P(('groups', 'wide')), parts along dimension 0, may hold values from -6 to 6
- cache_values: bfloat16 [32, 2048, 256], P(('groups', 'wide')), parts along dimension 0, may hold values from -6 to 6
- cache_len: int32 [32], P('groups'), parts along dimension 0, may hold values from 1 to 2048, 16384 in all
- o_weight: bfloat16 [2048, 2048], P('wide'), may hold values from -0.75 to 0.75
- norm_gain: float32 [2048], replicated, may hold values from 0.5 to 2
- expert_ids: int32 [4096, 8], P(('groups', 'wide')), parts along dimension 0, may hold values from 0 to 15, all different within a row; in each aligned block of 128 rows (0 to 127, 128 to 255, ...) at most 72 rows name the same one
- gate_raw: float32 [4096, 8], P(('groups', 'wide')), parts along dimension 0, may hold values from 0.1 to 1
- w_gate: bfloat16 [16, 2048, 768], P('wide'), may hold values from -0.125 to 0.125
- w_up: bfloat16 [16, 2048, 768], P('wide'), may hold values from -0.125 to 0.125
- w_down: bfloat16 [16, 768, 2048], P('wide'), may hold values from -0.4375 to 0.4375
Outputs:
- layer_out: bfloat16 [4096, 2048], P(('groups', 'wide')), parts along dimension 0
The draws below stay inside these ranges and needn't reach their ends.
There are 2 independent parts, one for each index of `groups`. The reference program is written for one: setup_inputs(seed, part) draws one part's arguments, and reference() takes and returns one part's arrays. A program takes and returns all parts, laid end to end along the dimension named above; an argument that names none is the same for every part. Nothing has to cross between parts.
Inputs may be any that keep to these rules, and one draw needn't show every extreme that they name: `cache_len`: each span's cache holds 1 or more positions; in every part some span has a full cache of 2048 positions and the lengths sum to 16384. `expert_ids`: each token names 8 different experts; among the 128 tokens of one span no expert is named more than 72 times, and in every draw some span names some expert exactly 72 times.
All inputs are finite; a program needn't handle non-finite values.
Results may differ from the reference program's by a relative error of at most 0.01.
Values may be sent and summed in bfloat16 or wider, within the bound.
No kernel may reach another device: no remote copies, remote signals or barrier semaphores. Data moves between devices by JAX's collectives and lax.ppermute only.
A program may use at most 128 MiB of HBM per device.

```python
import math
import jax
import jax.numpy as jnp
import numpy as np
from jax import lax

D = 2048
HEADS = 16
KV_HEADS = 2
HEAD = 128
FF = 768
TOPK = 8
SPAN = 128
CACHE = 2048
EXPERTS = 16
TOKENS = 2048
CAP = 72
N_WIDE = 16


def attention_fields(key):
    cached = jnp.clip(jax.random.normal(jax.random.fold_in(key, 11), (N_WIDE, CACHE, KV_HEADS * HEAD), jnp.float32), -4.5, 4.5)
    fresh = jnp.clip(jax.random.normal(jax.random.fold_in(key, 12), (TOKENS, KV_HEADS * HEAD), jnp.float32), -6.0, 6.0)
    asked = jnp.clip(jax.random.normal(jax.random.fold_in(key, 13), (TOKENS, HEADS * HEAD), jnp.float32), -6.0, 6.0)
    return (cached, fresh, asked)


def draw_cache_keys(key, part):
    return attention_fields(key)[0].astype(jnp.bfloat16)


def draw_new_keys(key, part):
    return attention_fields(key)[1].astype(jnp.bfloat16)


def draw_queries(key, part):
    return attention_fields(key)[2].astype(jnp.bfloat16)


def shard_levels(key, dims, shards, smallest, top_value):
    factor_of = 1.0
    for dim, blocks in shards:
        steps = jax.random.uniform(jax.random.fold_in(jax.random.fold_in(key, 6), dim), (blocks,), jnp.float32, smallest / len(shards), top_value / len(shards))
        factor_of = factor_of * jnp.repeat(jnp.exp(steps), dims[dim] // blocks).reshape((-1,) + (1,) * (len(dims) - 1 - dim))
    return factor_of


def length_profile(amount, total, most, slope):
    loads = [(1 << 20) // math.isqrt(grade ** slope) + 1 for grade in range(2, amount + 1)]
    rest, given = total - most - (amount - 1), [1] * (amount - 1)
    while rest > 0:
        movable = [i for i in range(amount - 1) if given[i] < most]
        whole, budget = sum([loads[i] for i in movable]), rest
        for i in movable:
            addition = min(most - given[i], max(1, budget * loads[i] // whole), rest)
            given[i] = given[i] + addition
            rest = rest - addition
    return np.array([most] + given)


def uneven(key, number_of, total, bound, slope):
    if number_of == 2:
        one = jax.random.randint(key, (), max(1, total - bound), min(bound, total - 1) + 1)
        return jnp.stack([one, total - one])
    tallies = jnp.asarray(length_profile(number_of, total, bound, slope), jnp.int32)
    pairs = (number_of - 1) // 2
    source_of, receiver = tallies[1:1 + 2 * pairs:2], tallies[2:2 + 2 * pairs:2]
    room = jnp.minimum(source_of - 1, bound - receiver)
    passed = jax.random.randint(jax.random.fold_in(key, 1), (pairs,), 0, 1 << 20) % (room + 1)
    tallies = tallies.at[1:1 + 2 * pairs:2].set(source_of - passed).at[2:2 + 2 * pairs:2].set(receiver + passed)
    return tallies[jax.random.permutation(jax.random.fold_in(key, 2), number_of)]


def routed_block(rng, own, number, rows, amount, top, most, slope):
    order = jax.random.permutation(rng, amount)
    packed, usual = portions_of(amount, rows * top, most, slope, True), portions_of(amount, rows * top, most, slope, False)
    places = jnp.arange(amount)

    def named(sizes, turn):
        used = int((sizes > 0).sum())
        fixed = max(1, used // 4)
        moved = fixed + (places - fixed + turn * (used - fixed)) % max(1, amount - fixed)
        return jnp.zeros((amount,), jnp.int32).at[order[jnp.where(places < fixed, places, moved)]].set(jnp.asarray(sizes, jnp.int32))

    sizes = jnp.where(number % 4 == 0, named(packed, number // 4), named(usual, number - number // 4 - 1))
    mixed = jax.random.permutation(jax.random.fold_in(own, 3), amount)
    source_of, receiver = mixed[0:amount // 2 * 2:2], mixed[1:amount // 2 * 2:2]
    margin = jnp.minimum(sizes[source_of] - 1, most - sizes[receiver]) // 2
    margin = jnp.where((source_of == order[0]) | (receiver == order[0]) | (sizes[receiver] == 0), 0, jnp.maximum(margin, 0))
    moved = jax.random.randint(jax.random.fold_in(own, 4), (amount // 2,), 0, 1 << 20) % (margin + 1)
    sizes = sizes.at[source_of].add(-moved).at[receiver].add(moved)
    members = jnp.searchsorted(jnp.cumsum(sizes), jnp.arange(rows * top), side="right").astype(jnp.int32)
    grid = members.reshape(top, rows).T
    grid = grid[jax.random.permutation(jax.random.fold_in(own, 1), rows)]
    turn = jax.random.randint(jax.random.fold_in(own, 2), (rows, 1), 0, top)
    return jnp.take_along_axis(grid, (jnp.arange(top)[None, :] + turn) % top, axis=1)


def portions_of(count, total, reach, skew, full):
    weights = [(1 << 20) // math.isqrt(rank ** skew) + 1 for rank in range(1, count + 1)]
    largest = reach if full else min(reach, max(-(-total // count), total * weights[0] // sum(weights)))
    least = 1 if total - largest >= count - 1 else 0
    counts, rest = [largest] + [least] * (count - 1), total - largest - least * (count - 1)
    while rest > 0:
        free = [i for i in range(1, count) if counts[i] < largest] or [i for i in range(1, count) if counts[i] < reach]
        pool, budget = sum([weights[i] for i in free]), rest
        for i in free:
            addition = min(reach - counts[i], max(1, budget * weights[i] // pool), rest)
            counts[i] = counts[i] + addition
            rest = rest - addition
    return np.array(counts)


def gaussian(stream_key, dims, spread, limit, split=(), dtype=jnp.bfloat16):
    entries = jax.random.normal(stream_key, dims, jnp.float32) * spread
    if len(split) > 0:
        entries = shard_levels(stream_key, dims, split, -0.22, 0.18) * entries
    return jnp.clip(entries, min=-limit, max=limit).astype(dtype)


def setup_inputs(seed: int = 0, part: int = 0) -> dict:
    streams_of = jax.random.split(jax.random.key(seed), 15)
    part_keys = jax.random.split(jax.random.fold_in(streams_of[14], part), 15)
    residual = gaussian(part_keys[0], (TOKENS, D), 1.0, 6.0, ((0, 16),))
    queries = draw_queries(jax.random.fold_in(jax.random.fold_in(streams_of[14], part), 71), part)
    new_keys = draw_new_keys(jax.random.fold_in(jax.random.fold_in(streams_of[14], part), 71), part)
    new_values = gaussian(part_keys[3], (TOKENS, KV_HEADS * HEAD), 1.0, 6.0, ((0, 16),))
    cache_keys = draw_cache_keys(jax.random.fold_in(jax.random.fold_in(streams_of[14], part), 71), part)
    cache_values = gaussian(part_keys[5], (N_WIDE, CACHE, KV_HEADS * HEAD), 1.0, 6.0, ((0, 16),))
    cache_len = uneven(part_keys[6], N_WIDE, N_WIDE * CACHE // 2, CACHE, 2).astype(jnp.int32)
    o_weight = gaussian(streams_of[7], (HEADS * HEAD, D), (D // 32) ** -0.5, 0.75, ((0, 16),))
    norm_gain = jnp.clip(jnp.exp(jax.random.uniform(streams_of[8], (D,), jnp.float32, math.log(0.5), math.log(2.0))), 0.5, 2.0)
    expert_ids_keys = jax.random.split(jax.random.fold_in(part_keys[9], 1), TOKENS // SPAN)
    expert_ids_turns = jax.random.permutation(jax.random.fold_in(part_keys[9], 3), TOKENS // SPAN)
    expert_ids = jax.vmap(lambda own, number: routed_block(jax.random.fold_in(part_keys[9], 2), own, number, SPAN, EXPERTS, TOPK, CAP, 1))(expert_ids_keys, expert_ids_turns).reshape((TOKENS, TOPK))
    gate_raw = jnp.clip(jnp.exp(math.log(1.0) - 2.3025851 * jax.random.uniform(part_keys[10], (TOKENS, TOPK), jnp.float32) ** shard_levels(part_keys[10], (TOKENS, TOPK), ((0, 16),), -0.2, 0.2)), 0.1, 1.0)
    w_gate = gaussian(streams_of[11], (EXPERTS, D, FF), D ** -0.5, 0.125, ((0, 16),))
    w_up = gaussian(streams_of[12], (EXPERTS, D, FF), D ** -0.5, 0.125, ((0, 16),))
    w_down = gaussian(streams_of[13], (EXPERTS, FF, D), (FF // 4) ** -0.5, 0.4375, ((0, 16),))
    return {"residual": residual, "queries": queries, "new_keys": new_keys, "new_values": new_values, "cache_keys": cache_keys, "cache_values": cache_values, "cache_len": cache_len, "o_weight": o_weight, "norm_gain": norm_gain, "expert_ids": expert_ids, "gate_raw": gate_raw, "w_gate": w_gate, "w_up": w_up, "w_down": w_down}


def attend_span(inputs):
    query_rows, key_new, value_new, key_cache, value_cache, length = inputs
    group_size = HEADS // KV_HEADS
    query_four = query_rows.astype(jnp.float32).reshape(SPAN, KV_HEADS, group_size, HEAD)
    key_all = jnp.concatenate([key_cache, key_new], axis=0).astype(jnp.float32).reshape(CACHE + SPAN, KV_HEADS, HEAD)
    value_all = jnp.concatenate([value_cache, value_new], axis=0).astype(jnp.float32).reshape(CACHE + SPAN, KV_HEADS, HEAD)
    scores = jnp.einsum('tgrd,kgd->grtk', query_four, key_all) * HEAD ** (-0.5)
    positions = jnp.arange(CACHE + SPAN).astype(jnp.int32)
    token_rows = jnp.arange(SPAN).astype(jnp.int32)
    visible = jnp.where(positions[None, :] < CACHE, positions[None, :] < length, positions[None, :] - CACHE <= token_rows[:, None])
    scores = jnp.where(visible[None, None], scores, jnp.float32(-1e+30))
    row_max = lax.optimization_barrier(jnp.max(scores, axis=-1, keepdims=True))
    weights = jnp.exp(scores - row_max)
    denominator = lax.optimization_barrier(jnp.sum(weights, axis=-1))
    rounded = lax.optimization_barrier(weights.astype(jnp.bfloat16)).astype(jnp.float32)
    numerator = jnp.einsum('grtk,kgd->grtd', rounded, value_all)
    output = numerator / denominator[..., None]
    return jnp.transpose(output, (2, 0, 1, 3)).reshape(SPAN, HEADS * HEAD).astype(jnp.bfloat16)

def reference(residual, queries, new_keys, new_values, cache_keys, cache_values, cache_len, o_weight, norm_gain, expert_ids, gate_raw, w_gate, w_up, w_down):
    attn = lax.map(attend_span, (queries.reshape(N_WIDE, SPAN, HEADS * HEAD), new_keys.reshape(N_WIDE, SPAN, KV_HEADS * HEAD), new_values.reshape(N_WIDE, SPAN, KV_HEADS * HEAD), cache_keys, cache_values, cache_len))
    attn = attn.reshape(TOKENS, HEADS * HEAD)
    projected = jnp.dot(attn, o_weight, preferred_element_type=jnp.float32)
    mixed = residual.astype(jnp.float32) + projected
    normed = (mixed * lax.rsqrt(lax.optimization_barrier(jnp.mean(mixed * mixed, axis=-1, keepdims=True)) + 1e-06) * norm_gain).astype(jnp.bfloat16)
    shares = gate_raw / lax.optimization_barrier(jnp.sum(gate_raw, axis=-1, keepdims=True))
    flat_ids = expert_ids.reshape(N_WIDE, SPAN * TOPK)
    one_hot = (flat_ids[..., None] == jnp.arange(EXPERTS).astype(jnp.int32)[None, None, :]).astype(jnp.int32)
    ranks = (lax.optimization_barrier(jnp.sum(jnp.cumsum(one_hot, axis=1) * one_hot, axis=-1)) - 1).astype(jnp.int32)
    source = jnp.arange(N_WIDE).astype(jnp.int32)[:, None]
    destination = (flat_ids * (N_WIDE * CAP) + source * CAP + ranks).astype(jnp.int32).reshape(-1)
    global_tokens = (source * SPAN + (jnp.arange(SPAN * TOPK).astype(jnp.int32) // TOPK)[None, :]).astype(jnp.int32).reshape(-1)
    token_table = jnp.full((EXPERTS * N_WIDE * CAP,), TOKENS, jnp.int32).at[destination].set(global_tokens).reshape(EXPERTS, N_WIDE * CAP)
    share_table = jnp.zeros((EXPERTS * N_WIDE * CAP,), jnp.float32).at[destination].set(shares.reshape(-1)).reshape(EXPERTS, N_WIDE * CAP)
    padded = jnp.concatenate([normed, jnp.zeros((1, D), jnp.bfloat16)], axis=0)

    def expert_step(carry, inputs):
        table_row, share_row, gate_w, up_w, down_w = inputs
        rows_in = padded[table_row]
        gate_part = jnp.dot(rows_in, gate_w, preferred_element_type=jnp.float32)
        up_part = jnp.dot(rows_in, up_w, preferred_element_type=jnp.float32)
        activated = (jax.nn.silu(gate_part) * up_part).astype(jnp.bfloat16)
        expert_rows = jnp.dot(activated, down_w, preferred_element_type=jnp.float32).astype(jnp.bfloat16)
        carry = carry.at[table_row].add(expert_rows.astype(jnp.float32) * share_row[:, None])
        return (carry, None)
    routed, unused = lax.scan(expert_step, jnp.zeros((TOKENS + 1, D), jnp.float32), (token_table, share_table, w_gate, w_up, w_down))
    return (mixed + routed[:TOKENS]).astype(jnp.bfloat16)
```

```python
import functools

import jax
import jax.numpy as jnp
from jax import lax
from jax.experimental import pallas as pl
from jax.experimental.pallas import tpu as pltpu
from jax.sharding import PartitionSpec as P

HEAD = 128
KEY_BLOCK = 512
ROW_BLOCK = 256
LOG2E = 1.4426950408889634
NEG = -1e30
MIB = 1 << 20

VMEM = pl.BlockSpec(memory_space=pltpu.VMEM)
SMEM = pl.BlockSpec(memory_space=pltpu.SMEM)
ANY = pl.BlockSpec(memory_space=pl.ANY)


def dot(a, b):
    return jnp.dot(a, b, preferred_element_type=jnp.float32)


def attention_kernel(len_ref, q_ref, nk_ref, nv_ref, k_ref, v_ref, o_ref):
    tokens = q_ref.shape[0]
    heads = q_ref.shape[1] // HEAD
    per_chunk = ROW_BLOCK // tokens
    length = len_ref[0]
    blocks = (length + KEY_BLOCK - 1) // KEY_BLOCK
    scale = jnp.float32(HEAD**-0.5 * LOG2E)

    def scores_of(q, k):
        return lax.dot_general(q, k, (((1,), (1,)), ((), ())), preferred_element_type=jnp.float32)

    for chunk in range(heads // per_chunk):
        cols = [pl.ds((chunk * per_chunk + i) * HEAD, HEAD) for i in range(per_chunk)]
        q = jnp.concatenate([q_ref[:, c] for c in cols], axis=0)

        def step(s, state, v):
            m, l, acc = state
            new_m = jnp.maximum(m, jnp.max(s, axis=1, keepdims=True))
            w = jnp.exp2((s - new_m) * scale)
            fade = jnp.exp2((m - new_m) * scale)
            l = l * fade + jnp.sum(w, axis=1, keepdims=True)
            acc = acc * fade + dot(w.astype(jnp.bfloat16), v)
            return new_m, l, acc

        s = scores_of(q, nk_ref[...])
        row = lax.broadcasted_iota(jnp.int32, s.shape, 0) % tokens
        col = lax.broadcasted_iota(jnp.int32, s.shape, 1)
        s = jnp.where(col <= row, s, NEG)
        m = jnp.max(s, axis=1, keepdims=True)
        w = jnp.exp2((s - m) * scale)
        state = (m, jnp.sum(w, axis=1, keepdims=True), dot(w.astype(jnp.bfloat16), nv_ref[...]))

        def body(i, state):
            rows = pl.ds(pl.multiple_of(i * KEY_BLOCK, KEY_BLOCK), KEY_BLOCK)
            s = scores_of(q, k_ref[rows, :])
            pos = i * KEY_BLOCK + lax.broadcasted_iota(jnp.int32, s.shape, 1)
            s = jnp.where(pos < length, s, NEG)
            return step(s, state, v_ref[rows, :])

        m, l, acc = lax.fori_loop(0, blocks, body, state)
        out = (acc / l).astype(jnp.bfloat16)
        for i in range(per_chunk):
            o_ref[:, cols[i]] = out[i * tokens : (i + 1) * tokens, :]


def attention(length, queries, new_keys, new_values, keys, values):
    tokens, width = queries.shape
    kv_heads = new_keys.shape[1] // HEAD
    group = width // kv_heads
    cache = keys.shape[0]
    return pl.pallas_call(
        attention_kernel,
        grid=(kv_heads,),
        in_specs=[
            SMEM,
            pl.BlockSpec((tokens, group), lambda g: (0, g)),
            pl.BlockSpec((tokens, HEAD), lambda g: (0, g)),
            pl.BlockSpec((tokens, HEAD), lambda g: (0, g)),
            pl.BlockSpec((cache, HEAD), lambda g: (0, g)),
            pl.BlockSpec((cache, HEAD), lambda g: (0, g)),
        ],
        out_specs=pl.BlockSpec((tokens, group), lambda g: (0, g)),
        out_shape=jax.ShapeDtypeStruct((tokens, width), jnp.bfloat16),
        compiler_params=pltpu.CompilerParams(vmem_limit_bytes=40 * MIB),
        cost_estimate=pl.CostEstimate(
            flops=4 * tokens * width * cache,
            bytes_accessed=4 * cache * HEAD * kv_heads,
            transcendentals=tokens * width // HEAD * cache,
        ),
        name="attention",
    )(length, queries, new_keys, new_values, keys, values)


def projection_kernel(n_blocks, base_ref, mine_ref, peer_ref, *refs):
    w_refs = refs[: n_blocks + 1]
    own_ref, other_ref, left, weight, sems = refs[n_blocks + 1 :]
    tokens = mine_ref.shape[0]
    rows = weight.shape[0] // n_blocks // 2
    half = weight.shape[1] // 2
    copies = []
    for b in range(n_blocks + 1):
        for part in range(2):
            at = pl.multiple_of(base_ref[2 * min(b, n_blocks - 1) + part], rows)
            src = w_refs[b].at[pl.ds(part * rows, rows)]
            if b < n_blocks - 1:
                dst = weight.at[pl.ds(at, rows)]
            else:
                dst = weight.at[pl.ds(at, rows), pl.ds((b - n_blocks + 1) * half, half)]
            copies.append(pltpu.make_async_copy(src, dst, sems.at[2 * b + part]))
            copies[-1].start()
    left[0:tokens] = mine_ref[...]
    left[tokens : 2 * tokens] = peer_ref[...]
    for copy in copies:
        copy.wait()
    step = 256

    def body(i, carry):
        cols = pl.ds(pl.multiple_of(i * step, step), step)
        both = dot(left[...], weight[:, cols])
        own_ref[:, cols] = both[:tokens]
        other_ref[:, cols] = both[tokens:]
        return carry

    lax.fori_loop(0, weight.shape[1] // step, body, 0)


def projection(bases, mine, peer, blocks):
    tokens, width = mine.shape
    n_blocks = len(blocks) - 1
    cols = blocks[0].shape[1]
    out = jax.ShapeDtypeStruct((tokens, cols), jnp.float32)
    return pl.pallas_call(
        functools.partial(projection_kernel, n_blocks),
        in_specs=[SMEM, VMEM, VMEM] + [ANY] * len(blocks),
        out_specs=[VMEM, VMEM],
        out_shape=[out, out],
        scratch_shapes=[
            pltpu.VMEM((2 * tokens, width), jnp.bfloat16),
            pltpu.VMEM((width, cols), jnp.bfloat16),
            pltpu.SemaphoreType.DMA((2 * n_blocks + 2,)),
        ],
        compiler_params=pltpu.CompilerParams(vmem_limit_bytes=40 * MIB),
        cost_estimate=pl.CostEstimate(
            flops=4 * tokens * width * cols, bytes_accessed=2 * width * cols, transcendentals=0
        ),
        name="projection",
    )(bases, mine, peer, *blocks)


def norm_kernel(core_ref, residual_ref, gain_ref, own_ref, recv_ref, mixed_ref, normed_ref):
    half = own_ref.shape[1]
    width = residual_ref.shape[1]
    core = core_ref[0]
    own_cols = pl.ds(pl.multiple_of(core * half, half), half)
    recv_cols = pl.ds(pl.multiple_of((1 - core) * half, half), half)
    a = residual_ref[:, own_cols].astype(jnp.float32) + own_ref[...]
    b = residual_ref[:, recv_cols].astype(jnp.float32) + recv_ref[...]
    mixed_ref[:, own_cols] = a
    mixed_ref[:, recv_cols] = b
    total = jnp.sum(a * a, axis=1, keepdims=True) + jnp.sum(b * b, axis=1, keepdims=True)
    factor = lax.rsqrt(total / width + 1e-06)
    normed_ref[:, own_cols] = (a * factor * gain_ref[:, own_cols]).astype(jnp.bfloat16)
    normed_ref[:, recv_cols] = (b * factor * gain_ref[:, recv_cols]).astype(jnp.bfloat16)


def mix_and_norm(core, residual, gain, own, recv):
    return pl.pallas_call(
        norm_kernel,
        in_specs=[SMEM, VMEM, VMEM, VMEM, VMEM],
        out_specs=[VMEM, VMEM],
        out_shape=[
            jax.ShapeDtypeStruct(residual.shape, jnp.float32),
            jax.ShapeDtypeStruct(residual.shape, jnp.bfloat16),
        ],
        compiler_params=pltpu.CompilerParams(vmem_limit_bytes=32 * MIB),
        name="mix_and_norm",
    )(core, residual, gain, own, recv)


def experts_kernel(pairs, n_in, n_out, slots, slot_rows, slot_cols, share_rows, *refs):
    x_refs = refs[:n_in]
    w_refs = refs[n_in : n_in + 6]
    out_refs = refs[n_in + 6 : n_in + 6 + n_out]
    xs, wg, wu, wd, rows_in, acc, scaled, x_sem, w_sem = refs[n_in + 6 + n_out :]
    depth = xs.shape[1]
    pair_tokens = xs.shape[0] // pairs
    block = pair_tokens // 2
    steps = wg.shape[0]
    ff = wg.shape[2]
    chunks = steps // 2

    x_copies = []
    at, col = 0, 0
    for i in range(n_in):
        wide = x_refs[i].shape[1]
        dst = xs.at[pl.ds(at, block), pl.ds(col, wide)]
        x_copies.append(pltpu.make_async_copy(x_refs[i], dst, x_sem.at[i]))
        x_copies[-1].start()
        col += wide
        if col == depth:
            at, col = at + block, 0
    for s in range(steps):
        e, f = s // chunks, s % chunks
        cut = pl.ds(f * ff, ff)
        pltpu.make_async_copy(w_refs[3 * e].at[:, cut], wg.at[s], w_sem.at[s, 0]).start()
        pltpu.make_async_copy(w_refs[3 * e + 1].at[:, cut], wu.at[s], w_sem.at[s, 1]).start()
        pltpu.make_async_copy(w_refs[3 * e + 2].at[cut, :], wd.at[s], w_sem.at[s, 2]).start()
    for copy in x_copies:
        copy.wait()

    step_cols = 512
    shares = []
    for p in range(pairs):
        row = lax.broadcasted_iota(jnp.int32, (2 * slots, pair_tokens), 0)
        first = row == slot_rows[p, 0:1, :]
        second = row - slots == slot_rows[p, 1:2, :]
        pick = jnp.where(first | second, 1.0, 0.0).astype(jnp.bfloat16)
        weight = jnp.where(first, share_rows[p, 0:1, :], 0.0) + jnp.where(
            second, share_rows[p, 1:2, :], 0.0
        )
        shares.append(jnp.sum(weight, axis=1, keepdims=True))

        def gather(i, carry, p=p, pick=pick):
            cols = pl.ds(pl.multiple_of(i * step_cols, step_cols), step_cols)
            got = dot(pick, xs[p * pair_tokens : (p + 1) * pair_tokens, cols]).astype(jnp.bfloat16)
            rows_in[0, p * slots : (p + 1) * slots, cols] = got[:slots]
            rows_in[1, p * slots : (p + 1) * slots, cols] = got[slots:]
            return carry

        lax.fori_loop(0, depth // step_cols, gather, 0)

    def expert(s, carry):
        e = s // chunks
        for k, ref in enumerate((wg, wu, wd)):
            pltpu.make_async_copy(ref.at[s], ref.at[s], w_sem.at[s, k]).wait()
        x = rows_in[e]
        gate = dot(x, wg[s])
        up = dot(x, wu[s])
        act = (gate / (1.0 + jnp.exp(-gate)) * up).astype(jnp.bfloat16)

        @pl.when(s % chunks == 0)
        def _():
            acc[e] = dot(act, wd[s])

        @pl.when(s % chunks != 0)
        def _():
            acc[e] += dot(act, wd[s])

        return carry

    lax.fori_loop(0, steps, expert, 0)

    at, col, o = 0, 0, 0
    for p in range(pairs):
        for e in range(2):
            part = shares[p][e * slots : (e + 1) * slots]
            scaled[e * slots : (e + 1) * slots, :] = (
                acc[e, p * slots : (p + 1) * slots, :] * part
            ).astype(jnp.bfloat16)
        lane = lax.broadcasted_iota(jnp.int32, (pair_tokens, 2 * slots), 1)
        back = (lane == slot_cols[p, :, 0:1]) | (lane - slots == slot_cols[p, :, 1:2])
        back = jnp.where(back, 1.0, 0.0).astype(jnp.bfloat16)
        for b in range(2):
            start = 0
            while start < depth:
                wide = out_refs[o].shape[1]

                def combine(i, carry, o=o, start=start, b=b, back=back):
                    src = pl.ds(pl.multiple_of(start + i * step_cols, step_cols), step_cols)
                    dst = pl.ds(pl.multiple_of(i * step_cols, step_cols), step_cols)
                    out_refs[o][:, dst] = dot(
                        back[b * block : (b + 1) * block], scaled[:, src]
                    ).astype(jnp.bfloat16)
                    return carry

                lax.fori_loop(0, wide // step_cols, combine, 0)
                start += wide
                o += 1


def experts(slots, slot_rows, slot_cols, share_rows, x_parts, weights, out_widths):
    pairs = slot_rows.shape[0]
    pair_tokens = slot_rows.shape[2]
    block = pair_tokens // 2
    depth, hidden = weights[0].shape
    ff = 256 if hidden % 256 == 0 else hidden
    chunks = hidden // ff
    n_in, n_out = len(x_parts), len(out_widths)
    return pl.pallas_call(
        functools.partial(experts_kernel, pairs, n_in, n_out, slots),
        in_specs=[VMEM, VMEM, VMEM] + [ANY] * (n_in + 6),
        out_specs=[VMEM] * n_out,
        out_shape=[jax.ShapeDtypeStruct((block, w), jnp.bfloat16) for w in out_widths],
        scratch_shapes=[
            pltpu.VMEM((pairs * pair_tokens, depth), jnp.bfloat16),
            pltpu.VMEM((2 * chunks, depth, ff), jnp.bfloat16),
            pltpu.VMEM((2 * chunks, depth, ff), jnp.bfloat16),
            pltpu.VMEM((2 * chunks, ff, depth), jnp.bfloat16),
            pltpu.VMEM((2, pairs * slots, depth), jnp.bfloat16),
            pltpu.VMEM((2, pairs * slots, depth), jnp.float32),
            pltpu.VMEM((2 * slots, depth), jnp.bfloat16),
            pltpu.SemaphoreType.DMA((n_in,)),
            pltpu.SemaphoreType.DMA((2 * chunks, 3)),
        ],
        compiler_params=pltpu.CompilerParams(vmem_limit_bytes=56 * MIB),
        cost_estimate=pl.CostEstimate(
            flops=12 * pairs * slots * depth * hidden,
            bytes_accessed=12 * depth * hidden,
            transcendentals=0,
        ),
        name="experts",
    )(slot_rows, slot_cols, share_rows, *x_parts, *weights)


def permutations(devices):
    cores = 2
    rows = 2
    ring = devices // (cores * rows)

    def index(z, y, c):
        return (z % ring * rows + y) * cores + c

    places = [(z, y, c) for z in range(ring) for y in range(rows) for c in range(cores)]
    forward = [(index(z, y, c), index(z + 1, y, c)) for z, y, c in places]
    backward = [(index(z, y, c), index(z + ring - 1, y, c)) for z, y, c in places]
    across = [(index(z, y, c), index(z, 1 - y, c)) for z, y, c in places]
    cores_swap = [(index(z, y, c), index(z, y, 1 - c)) for z, y, c in places]
    return ring, forward, backward, across, cores_swap


def per_device(
    residual,
    queries,
    new_keys,
    new_values,
    cache_keys,
    cache_values,
    cache_len,
    o_weight,
    norm_gain,
    expert_ids,
    gate_raw,
    w_gate,
    w_up,
    w_down,
):
    devices = lax.axis_size("wide")
    me = lax.axis_index("wide")
    tokens, depth = residual.shape
    top = expert_ids.shape[1]
    half = depth // 2
    ring, forward, backward, across, cores_swap = permutations(devices)
    core = me % 2
    row = me // 2 % 2
    place = me // 4

    send_forward = functools.partial(lax.ppermute, axis_name="wide", perm=forward)
    send_backward = functools.partial(lax.ppermute, axis_name="wide", perm=backward)
    send_across = functools.partial(lax.ppermute, axis_name="wide", perm=across)
    send_core = functools.partial(lax.ppermute, axis_name="wide", perm=cores_swap)

    def gather_blocks(own):
        same, other = [own], []
        for r in range(1, ring):
            same.append(send_forward(same[-1]))
        for r in range(ring - 1):
            other.append(send_across(same[r]))
        cut = own.shape[1] // 2
        if ring > 1:
            last = [send_across(same[-1][:, :cut]), send_forward(other[-1][:, cut:])]
        else:
            last = [send_across(own[:, :cut]), send_across(own[:, cut:])]
        return same, other, last

    mine_w = [w_gate[0], w_up[0], w_down[0]]

    keep = lax.dynamic_slice_in_dim(o_weight, core * half, half, 1)
    give = lax.dynamic_slice_in_dim(o_weight, (1 - core) * half, half, 1)
    own_block = jnp.concatenate([keep, send_core(give)], axis=0)
    w_same, w_other, w_last = gather_blocks(own_block)
    peer_w = [send_core(w) for w in mine_w]

    shares = gate_raw / jnp.sum(gate_raw, axis=-1, keepdims=True)
    table = jnp.concatenate([expert_ids.astype(jnp.float32).T, shares.T], axis=0)
    tables = lax.all_gather(table, "wide", axis=0, tiled=False)
    offsets = jnp.arange(ring, dtype=jnp.int32)
    rings = (place - offsets) % ring
    same_src = rings * 2 + row
    other_src = rings * 2 + 1 - row
    cap = tokens * top // devices + max(2, tokens * top // (8 * devices))
    slots = -(-2 * cap // 16) * 16

    order = jnp.stack([same_src, other_src], axis=0).reshape(2, ring // 2, 2).transpose(1, 0, 2)
    picked = tables[(order * 2 + core).reshape(-1)]
    ids = picked[:, :top]
    served = jnp.stack([me, me ^ 1]).astype(jnp.float32)
    hit = ids[:, None] == served[None, :, None, None]
    share_te = jnp.sum(jnp.where(hit, picked[:, None, top:], 0.0), axis=2)
    mask = jnp.any(hit, axis=2)
    before = (jnp.arange(tokens)[:, None] < jnp.arange(tokens)[None, :]).astype(jnp.bfloat16)
    rank = dot(mask.astype(jnp.bfloat16).reshape(-1, tokens), before).reshape(mask.shape)
    base = (jnp.arange(mask.shape[0], dtype=jnp.int32) % 2 * cap)[:, None, None]
    slot = jnp.where(mask, rank.astype(jnp.int32) + base, -(1 << 20))

    def by_pair(a):
        return a.reshape(ring, 2, 2, tokens).transpose(0, 2, 1, 3).reshape(ring, 2, 2 * tokens)

    slot_rows = by_pair(slot)
    share_rows = by_pair(share_te)
    slot_cols = slot_rows.transpose(0, 2, 1)

    length = lax.dynamic_slice_in_dim(cache_len, me, 1, 0)
    attn = attention(length, queries, new_keys, new_values, cache_keys[0], cache_values[0])
    attn_peer = send_core(attn)

    first_of = jnp.concatenate([same_src, other_src]) * 2
    bases = jnp.stack([first_of + core, first_of + 1 - core], axis=1).reshape(-1)
    own_part, other_part = projection(
        bases * o_weight.shape[0], attn, attn_peer, w_same + w_other + w_last
    )
    mixed, normed = mix_and_norm(
        core.astype(jnp.int32).reshape(1),
        residual,
        norm_gain.reshape(1, -1),
        own_part,
        send_core(other_part),
    )

    x_same, x_other, x_last = gather_blocks(normed)

    p_parts, q_parts, q_last = [], [], None
    for r in range(0, ring, 2):
        final = r + 2 == ring
        second = x_last if final else [x_other[r + 1]]
        x_parts = [x_same[r], x_same[r + 1], x_other[r]] + second
        widths = [depth] * 3 + ([half, half] if final else [depth])
        outs = experts(
            slots,
            slot_rows[r : r + 2],
            slot_cols[r : r + 2],
            share_rows[r : r + 2],
            x_parts,
            mine_w + peer_w,
            widths,
        )
        p_parts += [outs[0], outs[1]]
        q_parts += [outs[2]]
        if final:
            q_last = [outs[3], outs[4]]
        else:
            q_parts += [outs[3]]

    def add(*terms):
        total = terms[0].astype(jnp.float32)
        for term in terms[1:]:
            total = total + term.astype(jnp.float32)
        return total.astype(jnp.bfloat16)

    from_row = send_across(q_last[0])
    from_ring = send_backward(q_last[1])
    moving = jnp.concatenate(
        [add(p_parts[-1][:, :half], from_row), p_parts[-1][:, half:]], axis=1
    )
    for r in range(ring - 2, -1, -1):
        q = q_parts[r]
        if r == ring - 2:
            q = jnp.concatenate([q[:, :half], add(q[:, half:], from_ring)], axis=1)
        from_row = send_across(q)
        came = send_backward(moving)
        if r > 0:
            moving = add(p_parts[r], from_row, came)
    total = (
        mixed
        + p_parts[0].astype(jnp.float32)
        + from_row.astype(jnp.float32)
        + came.astype(jnp.float32)
    )
    return total.astype(jnp.bfloat16)


def solution(mesh):
    placed = (
        P(("groups", "wide"), None),
        P(("groups", "wide"), None),
        P(("groups", "wide"), None),
        P(("groups", "wide"), None),
        P(("groups", "wide"), None, None),
        P(("groups", "wide"), None, None),
        P("groups"),
        P("wide", None),
        P(),
        P(("groups", "wide"), None),
        P(("groups", "wide"), None),
        P("wide", None, None),
        P("wide", None, None),
        P("wide", None, None),
    )
    return jax.shard_map(
        per_device,
        mesh=mesh,
        in_specs=placed,
        out_specs=P(("groups", "wide"), None),
        check_vma=False,
    )
```

```python
import functools

import jax
import jax.numpy as jnp
from jax import lax
from jax.experimental import pallas as pl
from jax.experimental.pallas import tpu as pltpu
from jax.sharding import PartitionSpec as P

HEAD = 128
KEY_BLOCK = 1024
LOG2E = 1.4426950408889634
NEG = -1e30
MIB = 1 << 20

VMEM = pl.BlockSpec(memory_space=pltpu.VMEM)
SMEM = pl.BlockSpec(memory_space=pltpu.SMEM)
ANY = pl.BlockSpec(memory_space=pl.ANY)


def dot(a, b):
    return jnp.dot(a, b, preferred_element_type=jnp.float32)


def attention_kernel(len_ref, q_ref, nk_ref, nv_ref, k_ref, v_ref, o_ref, q_all, scores, top, acc, total):
    tokens = q_ref.shape[0]
    heads = q_ref.shape[1] // HEAD
    cache = k_ref.shape[0]
    length = len_ref[0]
    blocks = (length + KEY_BLOCK - 1) // KEY_BLOCK
    scale = jnp.float32(HEAD**-0.5 * LOG2E)
    rows = heads * tokens

    for h in range(heads):
        q_all[h * tokens : (h + 1) * tokens, :] = q_ref[:, h * HEAD : (h + 1) * HEAD]

    def scores_of(k):
        return lax.dot_general(
            q_all[...], k, (((1,), (1,)), ((), ())), preferred_element_type=jnp.float32
        )

    def fold(x, op):
        parts = [x[:, i : i + HEAD] for i in range(0, x.shape[1], HEAD)]
        while len(parts) > 1:
            parts = [op(*parts[i : i + 2]) if i + 1 < len(parts) else parts[i] for i in range(0, len(parts), 2)]
        return parts[0]

    s = scores_of(nk_ref[...])
    row = lax.broadcasted_iota(jnp.int32, s.shape, 0) % tokens
    col = lax.broadcasted_iota(jnp.int32, s.shape, 1)
    s = jnp.where(col <= row, s, NEG)
    scores[:, cache:] = s
    top[...] = fold(s, jnp.maximum)

    def score(i, carry):
        at = pl.ds(pl.multiple_of(i * KEY_BLOCK, KEY_BLOCK), KEY_BLOCK)
        s = scores_of(k_ref[at, :])
        pos = lax.broadcasted_iota(jnp.int32, s.shape, 1)
        s = jnp.where(pos < length - i * KEY_BLOCK, s, NEG)
        scores[:, at] = s
        top[...] = jnp.maximum(top[...], fold(s, jnp.maximum))
        return carry

    lax.fori_loop(0, blocks, score, 0)
    best = jnp.max(top[...], axis=1, keepdims=True) * scale
    top[...] = jnp.broadcast_to(best, top.shape)

    def weigh(s):
        shift = jnp.concatenate([top[...]] * (s.shape[1] // HEAD), axis=1)
        return jnp.exp2(s * scale - shift)

    w = weigh(scores[:, cache:])
    total[...] = fold(w, jnp.add)
    acc[...] = dot(w.astype(jnp.bfloat16), nv_ref[...])

    def add_block(i, carry):
        at = pl.ds(pl.multiple_of(i * KEY_BLOCK, KEY_BLOCK), KEY_BLOCK)
        w = weigh(scores[:, at])
        total[...] += fold(w, jnp.add)
        acc[...] += dot(w.astype(jnp.bfloat16), v_ref[at, :])
        return carry

    lax.fori_loop(0, blocks, add_block, 0)
    out = (acc[...] / jnp.sum(total[...], axis=1, keepdims=True)).astype(jnp.bfloat16)
    for h in range(heads):
        o_ref[:, h * HEAD : (h + 1) * HEAD] = out[h * tokens : (h + 1) * tokens, :]


def attention(part, parts, length, queries, new_keys, new_values, keys, values):
    tokens, width = queries.shape
    kv_heads = new_keys.shape[1] // HEAD
    g = part * kv_heads // parts
    group = width // parts
    cache = keys.shape[0]
    rows = group // HEAD * tokens
    return pl.pallas_call(
        attention_kernel,
        grid=(1,),
        in_specs=[
            SMEM,
            pl.BlockSpec((tokens, group), lambda i: (0, part)),
            pl.BlockSpec((tokens, HEAD), lambda i: (0, g)),
            pl.BlockSpec((tokens, HEAD), lambda i: (0, g)),
            pl.BlockSpec((cache, HEAD), lambda i: (0, g)),
            pl.BlockSpec((cache, HEAD), lambda i: (0, g)),
        ],
        out_specs=pl.BlockSpec((tokens, group), lambda i: (0, 0)),
        out_shape=jax.ShapeDtypeStruct((tokens, group), jnp.bfloat16),
        scratch_shapes=[
            pltpu.VMEM((rows, HEAD), jnp.bfloat16),
            pltpu.VMEM((rows, cache + tokens), jnp.float32),
            pltpu.VMEM((rows, HEAD), jnp.float32),
            pltpu.VMEM((rows, HEAD), jnp.float32),
            pltpu.VMEM((rows, HEAD), jnp.float32),
        ],
        compiler_params=pltpu.CompilerParams(vmem_limit_bytes=58 * MIB),
        cost_estimate=pl.CostEstimate(
            flops=20 * tokens * group * cache,
            bytes_accessed=4 * cache * HEAD,
            transcendentals=tokens * group // HEAD * cache,
        ),
        name="attention",
    )(length, queries, new_keys, new_values, keys, values)


def projection_kernel(n_pieces, n_blocks, base_ref, *refs):
    pieces, w_refs = refs[:n_pieces], refs[n_pieces : n_pieces + n_blocks + 1]
    outs = refs[n_pieces + n_blocks + 1 : -3]
    left, weight, sems = refs[-3:]
    tokens, group = pieces[0].shape
    rows = weight.shape[0] // n_blocks // 2
    half = weight.shape[1] // 2
    copies = []
    for b in range(n_blocks + 1):
        for part in range(2):
            at = pl.multiple_of(base_ref[2 * min(b, n_blocks - 1) + part], rows)
            src = w_refs[b].at[pl.ds(part * rows, rows)]
            if b < n_blocks - 1:
                dst = weight.at[pl.ds(at, rows)]
            else:
                dst = weight.at[pl.ds(at, rows), pl.ds((b - n_blocks + 1) * half, half)]
            copies.append(pltpu.make_async_copy(src, dst, sems.at[2 * b + part]))
            copies[-1].start()
    each = n_pieces // len(outs)
    for i in range(n_pieces):
        at = (i // each) * tokens
        left[at : at + tokens, (i % each) * group : (i % each + 1) * group] = pieces[i][...]
    for copy in copies:
        copy.wait()
    whole = dot(left[...], weight[...])
    for i, out in enumerate(outs):
        out[...] = whole[i * tokens : (i + 1) * tokens].astype(out.dtype)


def projection(bases, pieces, blocks, types):
    tokens, group = pieces[0].shape
    width = len(pieces) // len(types) * group
    n_blocks = len(blocks) - 1
    cols = blocks[0].shape[1]
    return pl.pallas_call(
        functools.partial(projection_kernel, len(pieces), n_blocks),
        in_specs=[SMEM] + [VMEM] * len(pieces) + [ANY] * len(blocks),
        out_specs=[VMEM] * len(types),
        out_shape=[jax.ShapeDtypeStruct((tokens, cols), t) for t in types],
        scratch_shapes=[
            pltpu.VMEM((len(types) * tokens, width), jnp.bfloat16),
            pltpu.VMEM((width, cols), jnp.bfloat16),
            pltpu.SemaphoreType.DMA((2 * n_blocks + 2,)),
        ],
        compiler_params=pltpu.CompilerParams(vmem_limit_bytes=58 * MIB),
        cost_estimate=pl.CostEstimate(
            flops=8 * tokens * width * cols, bytes_accessed=2 * width * cols, transcendentals=0
        ),
        name="projection",
    )(bases, *pieces, *blocks)


def norm_kernel(place_ref, residual_ref, gain_ref, *refs):
    parts, mixed_ref, normed_refs = refs[:-3], refs[-3], refs[-2:]
    cols, width = parts[0].shape[1], residual_ref.shape[1]
    total = 0.0
    for i, part in enumerate(parts):
        at = pl.ds(pl.multiple_of(place_ref[i], HEAD), cols)
        mixed = residual_ref[:, at].astype(jnp.float32) + part[...].astype(jnp.float32)
        mixed_ref[:, at] = mixed
        total = total + jnp.sum(mixed * mixed, axis=1, keepdims=True)
    factor = lax.rsqrt(total / width + 1e-06)
    half = width // 2
    for h, normed_ref in enumerate(normed_refs):
        at = slice(h * half, (h + 1) * half)
        normed_ref[...] = (mixed_ref[:, at] * factor * gain_ref[:, at]).astype(jnp.bfloat16)


def mix_and_norm(places, residual, gain, parts):
    return pl.pallas_call(
        norm_kernel,
        in_specs=[SMEM] + [VMEM] * (2 + len(parts)),
        out_specs=[VMEM] * 3,
        out_shape=[jax.ShapeDtypeStruct(residual.shape, jnp.float32)]
        + [jax.ShapeDtypeStruct((residual.shape[0], residual.shape[1] // 2), jnp.bfloat16)] * 2,
        compiler_params=pltpu.CompilerParams(vmem_limit_bytes=58 * MIB),
        name="mix_and_norm",
    )(places, residual, gain, *parts)


def finish_kernel(mixed_ref, *refs):
    out_ref = refs[-1]
    terms = (len(refs) - 1) // 2
    half = refs[0].shape[1]
    for h in range(2):
        cols = slice(h * half, (h + 1) * half)
        total = mixed_ref[:, cols]
        for ref in refs[h * terms : (h + 1) * terms]:
            total = total + ref[...].astype(jnp.float32)
        out_ref[:, cols] = total.astype(out_ref.dtype)


def finish(mixed, first, second):
    return pl.pallas_call(
        finish_kernel,
        in_specs=[VMEM] * (1 + len(first) + len(second)),
        out_specs=VMEM,
        out_shape=jax.ShapeDtypeStruct(mixed.shape, jnp.bfloat16),
        name="finish",
    )(mixed, *first, *second)


def routing_kernel(cap, served_ref, table_ref, rows_ref, cols_ref, shares_ref, mask):
    blocks, _, _, tokens = table_ref.shape
    for b in range(blocks):
        ids = table_ref[b, 0].astype(jnp.float32)
        share = table_ref[b, 1].astype(jnp.float32) + table_ref[b, 2].astype(jnp.float32)
        at = slice(b % 2 * tokens, (b % 2 + 1) * tokens)
        for e in range(2):
            hit = ids == served_ref[e].astype(jnp.float32)
            mask[2 * b + e : 2 * b + e + 1, :] = jnp.max(
                jnp.where(hit, 1.0, 0.0), axis=0, keepdims=True
            )
            shares_ref[b // 2, e : e + 1, at] = jnp.sum(
                jnp.where(hit, share, 0.0), axis=0, keepdims=True
            )
    first = lax.broadcasted_iota(jnp.int32, (tokens, tokens), 0)
    second = lax.broadcasted_iota(jnp.int32, (tokens, tokens), 1)
    before = jnp.where(first < second, 1.0, 0.0).astype(jnp.bfloat16)
    same = jnp.where(first == second, 1.0, 0.0).astype(jnp.bfloat16)
    there = mask[...]
    rank = dot(there.astype(jnp.bfloat16), before)
    line = lax.broadcasted_iota(jnp.int32, rank.shape, 0)
    slot = jnp.where(there > 0.5, rank + jnp.where(line // 2 % 2 == 1, float(cap), 0.0), -512.0)
    columns = lax.dot_general(
        same, slot.astype(jnp.bfloat16), (((1,), (1,)), ((), ())), preferred_element_type=jnp.float32
    )
    for b in range(blocks):
        at = slice(b % 2 * tokens, (b % 2 + 1) * tokens)
        lines = slice(2 * b, 2 * b + 2)
        rows_ref[b // 2, :, at] = slot[lines].astype(jnp.int32)
        cols_ref[b // 2, at, :] = columns[:, lines].astype(jnp.int32)


def routing(cap, served, table):
    blocks, _, _, tokens = table.shape
    pairs = blocks // 2
    rows = jax.ShapeDtypeStruct((pairs, 2, 2 * tokens), jnp.int32)
    return pl.pallas_call(
        functools.partial(routing_kernel, cap),
        in_specs=[SMEM, VMEM],
        out_specs=[VMEM] * 3,
        out_shape=[
            rows,
            jax.ShapeDtypeStruct((pairs, 2 * tokens, 2), jnp.int32),
            jax.ShapeDtypeStruct(rows.shape, jnp.float32),
        ],
        scratch_shapes=[pltpu.VMEM((2 * blocks, tokens), jnp.float32)],
        compiler_params=pltpu.CompilerParams(vmem_limit_bytes=16 * MIB),
        name="routing",
    )(served, table)


def fetch_kernel(*refs):
    count = (len(refs) - 2) // 2
    token, sems = refs[-2:]
    token[...] = jnp.zeros_like(token)
    copies = [
        pltpu.make_async_copy(refs[i], refs[count + i], sems.at[i]) for i in range(count)
    ]
    for copy in copies:
        copy.start()
    for copy in copies:
        copy.wait()


def fetch(arrays):
    arrays = [pltpu.with_memory_space_constraint(a, pltpu.HBM) for a in arrays]
    *there, token = pl.pallas_call(
        fetch_kernel,
        in_specs=[ANY] * len(arrays),
        out_specs=[VMEM] * (len(arrays) + 1),
        out_shape=[pltpu.VMEM(a.shape, a.dtype) for a in arrays]
        + [jax.ShapeDtypeStruct((8, HEAD), jnp.float32)],
        scratch_shapes=[pltpu.SemaphoreType.DMA((len(arrays),))],
        compiler_params=pltpu.CompilerParams(vmem_limit_bytes=24 * MIB),
        name="fetch",
    )(*arrays)
    return there, token


def experts_kernel(first_pair, pairs, n_in, n_out, slots, slot_rows, slot_cols, share_rows, *refs):
    x_refs = refs[:n_in]
    w_refs = refs[n_in : n_in + 6]
    out_refs = refs[n_in + 7 : n_in + 7 + n_out]
    xs, rows_in, act, scaled, x_sem = refs[n_in + 7 + n_out :]
    depth = xs.shape[1]
    pair_tokens = xs.shape[0] // pairs
    block = pair_tokens // 2
    hidden = act.shape[1]

    x_copies = []
    at, col = 0, 0
    for i in range(n_in):
        wide = x_refs[i].shape[1]
        dst = xs.at[pl.ds(at, block), pl.ds(col, wide)]
        x_copies.append(pltpu.make_async_copy(x_refs[i], dst, x_sem.at[i]))
        x_copies[-1].start()
        col += wide
        if col == depth:
            at, col = at + block, 0
    for copy in x_copies:
        copy.wait()

    shares = []
    for p in range(pairs):
        row = lax.broadcasted_iota(jnp.int32, (2 * slots, pair_tokens), 0)
        first = row == slot_rows[first_pair + p, 0:1, :]
        second = row - slots == slot_rows[first_pair + p, 1:2, :]
        pick = jnp.where(first | second, 1.0, 0.0).astype(jnp.bfloat16)
        weight = jnp.where(first, share_rows[first_pair + p, 0:1, :], 0.0) + jnp.where(
            second, share_rows[first_pair + p, 1:2, :], 0.0
        )
        shares.append(jnp.sum(weight, axis=1, keepdims=True))
        step = min(1024, depth)
        for c in range(0, depth, step):
            got = dot(pick, xs[p * pair_tokens : (p + 1) * pair_tokens, c : c + step])
            got = got.astype(jnp.bfloat16)
            rows_in[0, p * slots : (p + 1) * slots, c : c + step] = got[:slots]
            rows_in[1, p * slots : (p + 1) * slots, c : c + step] = got[slots:]

    for e in range(2):
        x = rows_in[e]
        gate = dot(x, w_refs[3 * e][...])
        up = dot(x, w_refs[3 * e + 1][...])
        act[...] = (gate / (1.0 + jnp.exp(-gate)) * up).astype(jnp.bfloat16)
        share = jnp.concatenate([s[e * slots : (e + 1) * slots] for s in shares], axis=0)
        y = (dot(act[...], w_refs[3 * e + 2][...]) * share).astype(jnp.bfloat16)
        for p in range(pairs):
            scaled[p, e * slots : (e + 1) * slots, :] = y[p * slots : (p + 1) * slots]

    o = 0
    for p in range(pairs):
        lane = lax.broadcasted_iota(jnp.int32, (pair_tokens, 2 * slots), 1)
        back = lane == slot_cols[first_pair + p, :, 0:1]
        back = back | (lane - slots == slot_cols[first_pair + p, :, 1:2])
        back = jnp.where(back, 1.0, 0.0).astype(jnp.bfloat16)
        place = []
        for b in range(2):
            start = 0
            while start < depth:
                place.append((b, start, out_refs[o]))
                start += out_refs[o].shape[1]
                o += 1
        step = min(1024, depth)
        for c in range(0, depth, step):
            got = dot(back, scaled[p, :, c : c + step]).astype(jnp.bfloat16)
            for b, start, ref in place:
                if start <= c < start + ref.shape[1]:
                    ref[:, c - start : c - start + step] = got[b * block : (b + 1) * block]


def experts(slots, first_pair, pairs, slot_rows, slot_cols, share_rows, x_parts, weights, out_widths):
    pair_tokens = slot_rows.shape[2]
    block = pair_tokens // 2
    depth, hidden = weights[0].shape
    n_in, n_out = len(x_parts), len(out_widths)
    return pl.pallas_call(
        functools.partial(experts_kernel, first_pair, pairs, n_in, n_out, slots),
        in_specs=[VMEM, VMEM, VMEM] + [ANY] * n_in + [VMEM] * 6 + [ANY],
        out_specs=[VMEM] * n_out,
        out_shape=[jax.ShapeDtypeStruct((block, w), jnp.bfloat16) for w in out_widths],
        scratch_shapes=[
            pltpu.VMEM((pairs * pair_tokens, depth), jnp.bfloat16),
            pltpu.VMEM((2, pairs * slots, depth), jnp.bfloat16),
            pltpu.VMEM((pairs * slots, hidden), jnp.bfloat16),
            pltpu.VMEM((pairs, 2 * slots, depth), jnp.bfloat16),
            pltpu.SemaphoreType.DMA((n_in,)),
        ],
        compiler_params=pltpu.CompilerParams(vmem_limit_bytes=32 * MIB),
        cost_estimate=pl.CostEstimate(
            flops=12 * pairs * slots * depth * hidden,
            bytes_accessed=12 * depth * hidden,
            transcendentals=0,
        ),
        name="experts",
    )(slot_rows, slot_cols, share_rows, *x_parts, *weights)


def permutations(devices):
    cores, rows = 2, 2
    ring = devices // (cores * rows)

    def index(z, y, c):
        return (z % ring * rows + y % rows) * cores + c % cores

    def shift(dz, dy=0, dc=0):
        return [
            (index(z, y, c), index(z + dz + ring, y + dy, c + dc))
            for z in range(ring)
            for y in range(rows)
            for c in range(cores)
        ]

    return ring, shift


def per_device(
    residual,
    queries,
    new_keys,
    new_values,
    cache_keys,
    cache_values,
    cache_len,
    o_weight,
    norm_gain,
    expert_ids,
    gate_raw,
    w_gate,
    w_up,
    w_down,
):
    devices = lax.axis_size("wide")
    replicas = lax.axis_size("groups")
    me = lax.axis_index("wide")
    tokens, depth = residual.shape
    top = expert_ids.shape[1]
    half = depth // 2
    ring, shift = permutations(devices)
    core = me % 2
    row = me // 2 % 2
    place = me // 4
    side = lax.axis_index("groups") % 2

    def sender(*by):
        return lambda x: lax.ppermute(x, "wide", shift(*by))

    def side_sender(*by):
        pairs = [
            (g * devices + a, (g ^ 1) * devices + b)
            for g in range(replicas)
            for a, b in shift(*by)
        ]
        return lambda x: lax.ppermute(x, ("groups", "wide"), pairs)

    send_forward, send_backward = sender(1), sender(-1)
    send_across, send_core = sender(0, 1), sender(0, 0, 1)
    send_side, send_corner = side_sender(0), side_sender(0, 0, 1)
    barrier = lax.optimization_barrier

    def gather_whole(own, beside):
        same, other = [own], []
        for r in range(1, ring):
            moved, crossed = send_forward(same[-1]), send_across(same[-1])
            new = beside[r - 1](same, other) if r <= len(beside) else {}
            moved, crossed, new = barrier((moved, crossed, new))
            kept.update(new)
            same.append(moved)
            other.append(crossed)
        cut = own.shape[1] // 2
        last = [send_across(same[-1][:, :cut]), send_forward(other[-1][:, cut:])]
        for step in beside[ring - 1 :]:
            last, new = barrier((last, step(same, other)))
            kept.update(new)
        return same, other, last

    def gather_halves(own, beside):
        same, other = [list(own)], []
        for r in range(1, ring):
            moved = [send_forward(h) for h in same[-1]]
            crossed = [send_across(h) for h in same[-1]]
            new = beside[r - 1](same, other) if r <= len(beside) else {}
            moved[0], crossed[0] = barrier((moved[0], crossed[0]))
            moved[1], crossed[1], new = barrier((moved[1], crossed[1], new))
            kept.update(new)
            same.append(moved)
            other.append(crossed)
        last = [send_across(same[-1][0]), send_forward(other[-1][1])]
        for step in beside[ring - 1 :]:
            last, new = barrier((last, step(same, other)))
            kept.update(new)
        other.append(last)
        return same, other

    kept = {}

    cols = depth // 4
    quarter = 2 * side + core
    keep = lax.dynamic_slice_in_dim(o_weight, quarter * cols, cols, 1)
    give = lax.dynamic_slice_in_dim(o_weight, (quarter ^ 1) * cols, cols, 1)
    shares = gate_raw / jnp.sum(gate_raw, axis=-1, keepdims=True)
    high = shares.astype(jnp.bfloat16)
    low = (shares - high.astype(jnp.float32)).astype(jnp.bfloat16)
    table = jnp.stack([expert_ids.astype(jnp.bfloat16), high, low]).transpose(0, 2, 1)
    table = table.reshape(-1, cols)
    table_rows = table.shape[0]
    table = jnp.pad(table, ((0, -table_rows % 16), (0, 0)))
    own_block = jnp.concatenate([keep, send_core(give), table], axis=0)
    length = lax.dynamic_slice_in_dim(cache_len, me, 1, 0)
    mine = [w_gate[0], w_up[0], w_down[0]]
    length, own_block, mine = barrier((length, own_block, mine))
    operands = (queries, new_keys, new_values, cache_keys[0], cache_values[0])

    def attend_first(same, other):
        return {"a0": attention(0, 2, length, *operands), "w0": send_core(mine[0])}

    def attend_second(same, other):
        begin, kept["a0"] = barrier((length, kept["a0"]))
        return {
            "a1": attention(1, 2, begin, *operands),
            "side0": send_side(kept["a0"]),
            "w1": send_core(mine[1]),
        }

    def swap_first(same, other):
        return {
            "side1": send_side(kept["a1"]),
            "core0": send_core(kept["a0"]),
            "w2": send_core(mine[2]),
        }

    def swap_second(same, other):
        return {
            "core1": send_core(kept["a1"]),
            "corner0": send_core(kept["side0"]),
            "corner1": send_core(kept["side1"]),
        }

    w_same, w_other, w_last = gather_whole(
        own_block, [attend_first, attend_second, swap_first, swap_second]
    )
    offsets = jnp.arange(ring, dtype=jnp.int32)
    rings = (place - offsets) % ring
    first_of = jnp.concatenate([rings * 2 + row, rings * 2 + 1 - row]) * 2
    bases = jnp.stack([first_of + core, first_of + 1 - core], axis=1).reshape(-1)
    pieces = [kept[name + str(g)] for name in ("a", "core", "side", "corner") for g in range(2)]
    own_part, core_part, side_part, corner_part = projection(
        bases * o_weight.shape[0],
        pieces,
        w_same + w_other + w_last,
        [jnp.float32, jnp.float32, jnp.bfloat16, jnp.bfloat16],
    )
    parts = [own_part, send_core(core_part), send_side(side_part), send_corner(corner_part)]
    places = jnp.stack([quarter, quarter ^ 1, quarter ^ 2, quarter ^ 3]).astype(jnp.int32) * cols
    mixed, *normed = mix_and_norm(places, residual, norm_gain.reshape(1, -1), parts)

    cap = tokens * top // devices + max(2, tokens * top // (8 * devices))
    slots = -(-2 * cap // 16) * 16

    def make_tables(same, other):
        rows = slice(own_block.shape[0] - table.shape[0], own_block.shape[0] - table.shape[0] + table_rows)
        blocks, same[0] = barrier((w_same + w_other + w_last, same[0]))
        tables = [b[rows] for b in blocks[:-2]]
        tables.append(jnp.concatenate([h[rows] for h in blocks[-2:]], axis=1))
        picked = jnp.stack(tables).reshape(2, ring // 2, 2, 3, top, tokens).transpose(1, 0, 2, 3, 4, 5)
        picked = picked.reshape(2 * ring, 3, top, tokens)
        names = ("slot_rows", "slot_cols", "share_rows")
        return dict(zip(names, routing(cap, jnp.stack([me, me ^ 1]), picked)))

    def load_weights(same, other):
        arrays = mine + [kept["w0"], kept["w1"], kept["w2"]]
        arrays, kept["slot_rows"], kept["slot_cols"] = barrier(
            (arrays, kept["slot_rows"], kept["slot_cols"])
        )
        weights, token = fetch(arrays)
        beside_weights.extend(weights)
        return {"token": token}

    beside_weights = []

    def serve(first, count, blocks):
        tables = [kept[name] for name in ("slot_rows", "slot_cols", "share_rows")]
        halves = [h for block in blocks for h in block]
        outs = experts(
            slots, first, count, *tables, halves, beside_weights + [kept["token"]], [half] * len(halves)
        )
        return [outs[i : i + 2] for i in range(0, len(outs), 2)]

    def nothing(same, other):
        return {}

    def serve_four(r):
        def step(same, other):
            p0, p1, q0, q1 = serve(r, 2, same[r : r + 2] + other[r : r + 2])
            return {("p", r): p0, ("p", r + 1): p1, ("q", r): q0, ("q", r + 1): q1}

        return step

    def serve_two(same, other):
        p0, p1 = serve(ring - 2, 1, same[-2:])
        return {("p", ring - 2): p0, ("p", ring - 1): p1}

    beside = [make_tables, load_weights]
    for r in range(0, ring - 2, 2):
        beside += [serve_four(r), nothing]
    beside[ring - 1 :] = [serve_two]
    x_same, x_other = gather_halves(normed, beside)
    q = [kept["q", r] for r in range(ring - 2)] + serve(ring - 1, 1, x_other[-2:])
    p = [kept["p", r] for r in range(ring)]

    def add(*terms):
        return sum(t.astype(jnp.float32) for t in terms).astype(jnp.bfloat16)

    r = ring - 1
    came = [None, send_backward(p[r][1])]
    extra = send_backward(q[r][1])
    crossed = [send_across(q[r][0]), None]
    later = [send_across(q[r - 1][0]), None]
    crossed[1] = send_across(add(q[r - 1][1], extra))
    came[0] = send_backward(add(p[r][0], crossed[0]))
    crossed[0] = later[0]
    for r in range(ring - 2, 0, -1):
        moving = [None, None]
        for h in (1, 0):
            total = add(p[r][h], came[h], crossed[h])
            total, behind = barrier((total, q[r - 1][h]))
            came[h] = send_backward(total)
            crossed[h] = send_across(behind)
    return finish(mixed, *[[p[0][h], came[h], crossed[h]] for h in range(2)])


def solution(mesh):
    placed = (
        P(("groups", "wide"), None),
        P(("groups", "wide"), None),
        P(("groups", "wide"), None),
        P(("groups", "wide"), None),
        P(("groups", "wide"), None, None),
        P(("groups", "wide"), None, None),
        P("groups"),
        P("wide", None),
        P(),
        P(("groups", "wide"), None),
        P(("groups", "wide"), None),
        P("wide", None, None),
        P("wide", None, None),
        P("wide", None, None),
    )
    return jax.shard_map(
        per_device,
        mesh=mesh,
        in_specs=placed,
        out_specs=P(("groups", "wide"), None),
        check_vma=False,
    )
```

```python
import functools

import jax
import jax.numpy as jnp
from jax import lax
from jax.experimental import pallas as pl
from jax.experimental.pallas import tpu as pltpu
from jax.sharding import PartitionSpec as P

HEAD = 128
KEY_BLOCK = 1024
LOG2E = 1.4426950408889634
NEG = -1e30
MIB = 1 << 20

VMEM = pl.BlockSpec(memory_space=pltpu.VMEM)
SMEM = pl.BlockSpec(memory_space=pltpu.SMEM)
ANY = pl.BlockSpec(memory_space=pl.ANY)


def dot(a, b):
    return jnp.dot(a, b, preferred_element_type=jnp.float32)


def attention_kernel(len_ref, q_ref, nk_ref, nv_ref, k_ref, v_ref, o_ref, q_all, scores, top, acc, total):
    tokens = q_ref.shape[0]
    heads = q_ref.shape[1] // HEAD
    cache = k_ref.shape[0]
    length = len_ref[0]
    blocks = (length + KEY_BLOCK - 1) // KEY_BLOCK
    scale = jnp.float32(HEAD**-0.5 * LOG2E)
    rows = heads * tokens

    for h in range(heads):
        q_all[h * tokens : (h + 1) * tokens, :] = q_ref[:, h * HEAD : (h + 1) * HEAD]

    def scores_of(k):
        return lax.dot_general(
            q_all[...], k, (((1,), (1,)), ((), ())), preferred_element_type=jnp.float32
        )

    def fold(x, op):
        parts = [x[:, i : i + HEAD] for i in range(0, x.shape[1], HEAD)]
        while len(parts) > 1:
            parts = [op(*parts[i : i + 2]) if i + 1 < len(parts) else parts[i] for i in range(0, len(parts), 2)]
        return parts[0]

    s = scores_of(nk_ref[...])
    row = lax.broadcasted_iota(jnp.int32, s.shape, 0) % tokens
    col = lax.broadcasted_iota(jnp.int32, s.shape, 1)
    s = jnp.where(col <= row, s, NEG)
    scores[:, cache:] = s
    top[...] = fold(s, jnp.maximum)

    def score(i, carry):
        at = pl.ds(pl.multiple_of(i * KEY_BLOCK, KEY_BLOCK), KEY_BLOCK)
        s = scores_of(k_ref[at, :])
        pos = lax.broadcasted_iota(jnp.int32, s.shape, 1)
        s = jnp.where(pos < length - i * KEY_BLOCK, s, NEG)
        scores[:, at] = s
        top[...] = jnp.maximum(top[...], fold(s, jnp.maximum))
        return carry

    lax.fori_loop(0, blocks, score, 0)
    best = jnp.max(top[...], axis=1, keepdims=True) * scale
    top[...] = jnp.broadcast_to(best, top.shape)

    def weigh(s):
        shift = jnp.concatenate([top[...]] * (s.shape[1] // HEAD), axis=1)
        return jnp.exp2(s * scale - shift)

    w = weigh(scores[:, cache:])
    total[...] = fold(w, jnp.add)
    acc[...] = dot(w.astype(jnp.bfloat16), nv_ref[...])

    def add_block(i, carry):
        at = pl.ds(pl.multiple_of(i * KEY_BLOCK, KEY_BLOCK), KEY_BLOCK)
        w = weigh(scores[:, at])
        total[...] += fold(w, jnp.add)
        acc[...] += dot(w.astype(jnp.bfloat16), v_ref[at, :])
        return carry

    lax.fori_loop(0, blocks, add_block, 0)
    out = (acc[...] / jnp.sum(total[...], axis=1, keepdims=True)).astype(jnp.bfloat16)
    for h in range(heads):
        o_ref[:, h * HEAD : (h + 1) * HEAD] = out[h * tokens : (h + 1) * tokens, :]


def attention(part, parts, length, queries, new_keys, new_values, keys, values):
    tokens, width = queries.shape
    kv_heads = new_keys.shape[1] // HEAD
    g = part * kv_heads // parts
    group = width // parts
    cache = keys.shape[0]
    rows = group // HEAD * tokens
    return pl.pallas_call(
        attention_kernel,
        grid=(1,),
        in_specs=[
            SMEM,
            pl.BlockSpec((tokens, group), lambda i: (0, part)),
            pl.BlockSpec((tokens, HEAD), lambda i: (0, g)),
            pl.BlockSpec((tokens, HEAD), lambda i: (0, g)),
            pl.BlockSpec((cache, HEAD), lambda i: (0, g)),
            pl.BlockSpec((cache, HEAD), lambda i: (0, g)),
        ],
        out_specs=pl.BlockSpec((tokens, group), lambda i: (0, 0)),
        out_shape=jax.ShapeDtypeStruct((tokens, group), jnp.bfloat16),
        scratch_shapes=[
            pltpu.VMEM((rows, HEAD), jnp.bfloat16),
            pltpu.VMEM((rows, cache + tokens), jnp.float32),
            pltpu.VMEM((rows, HEAD), jnp.float32),
            pltpu.VMEM((rows, HEAD), jnp.float32),
            pltpu.VMEM((rows, HEAD), jnp.float32),
        ],
        compiler_params=pltpu.CompilerParams(vmem_limit_bytes=58 * MIB),
        cost_estimate=pl.CostEstimate(
            flops=20 * tokens * group * cache,
            bytes_accessed=4 * cache * HEAD,
            transcendentals=tokens * group // HEAD * cache,
        ),
        name="attention",
    )(length, queries, new_keys, new_values, keys, values)


def projection_kernel(n_pieces, n_blocks, base_ref, *refs):
    pieces, w_refs = refs[:n_pieces], refs[n_pieces : n_pieces + n_blocks - 1]
    left_out, sum_out, weight, sems = refs[n_pieces + n_blocks - 1 :]
    tokens, group = pieces[0].shape
    rows = weight.shape[0] // n_blocks // 2
    each = left_out.shape[1] // group
    copies = []

    def begin(src, dst):
        copies.append(pltpu.make_async_copy(src, dst, sems.at[len(copies)]))
        copies[-1].start()

    for b in range(n_blocks - 1):
        for part in range(2):
            at = pl.multiple_of(base_ref[2 * b + part], rows)
            begin(w_refs[b].at[pl.ds(part * rows, rows)], weight.at[pl.ds(at, rows)])
    for i, piece in enumerate(pieces):
        dst = left_out.at[pl.ds(i // each * tokens, tokens), pl.ds(i % each * group, group)]
        begin(piece, dst)
    for part in range(2):
        at = pl.multiple_of(base_ref[2 * n_blocks - 2 + part], rows)
        weight[pl.ds(at, rows), :] = jnp.zeros((rows, weight.shape[1]), weight.dtype)
    for copy in copies:
        copy.wait()
    sum_out[...] = dot(left_out[...], weight[...])


def projection(bases, pieces, count, blocks):
    tokens, group = pieces[0].shape
    width = len(pieces) // count * group
    n_blocks = len(blocks) + 1
    cols = blocks[0].shape[1]
    return pl.pallas_call(
        functools.partial(projection_kernel, len(pieces), n_blocks),
        in_specs=[SMEM] + [ANY] * (len(pieces) + len(blocks)),
        out_specs=[VMEM] * 2,
        out_shape=[
            jax.ShapeDtypeStruct((count * tokens, width), jnp.bfloat16),
            jax.ShapeDtypeStruct((count * tokens, cols), jnp.float32),
        ],
        scratch_shapes=[
            pltpu.VMEM((width, cols), jnp.bfloat16),
            pltpu.SemaphoreType.DMA((2 * n_blocks - 2 + len(pieces),)),
        ],
        compiler_params=pltpu.CompilerParams(vmem_limit_bytes=24 * MIB),
        cost_estimate=pl.CostEstimate(
            flops=8 * tokens * width * cols, bytes_accessed=2 * width * cols, transcendentals=0
        ),
        name="projection",
    )(bases, *pieces, *blocks)


def complete_kernel(whole_tiles, base_ref, left_ref, sum_ref, first_ref, second_ref, *refs):
    outs, (piece, sems) = refs[:-2], refs[-2:]
    tokens = outs[0].shape[0]
    half = first_ref.shape[1]
    copies = []
    if whole_tiles:
        rows = piece.shape[1] // 2
        for part in range(2):
            at = pl.multiple_of(base_ref[part], rows)
            src = left_ref.at[:, pl.ds(at, rows)]
            dst = piece.at[:, pl.ds(part * rows, rows)]
            copies.append(pltpu.make_async_copy(src, dst, sems.at[part]))
    else:
        copies.append(pltpu.make_async_copy(left_ref, piece, sems.at[0]))
    for copy in copies:
        copy.start()
    for copy in copies:
        copy.wait()
    for h, w_ref in enumerate((first_ref, second_ref)):
        cols = slice(h * half, (h + 1) * half)
        whole = sum_ref[:, cols] + dot(piece[...], w_ref[...])
        for i, out in enumerate(outs):
            out[:, cols] = whole[i * tokens : (i + 1) * tokens].astype(out.dtype)


def complete(bases, rows, left, total, last, types):
    tokens = left.shape[0] // len(types)
    whole_tiles = rows % HEAD == 0
    if not whole_tiles:
        parts = [lax.dynamic_slice_in_dim(left, bases[i], rows, 1) for i in range(2)]
        left = jnp.concatenate(parts, axis=1)
    w_spec = pl.BlockSpec((2 * rows, last[0].shape[1]), lambda i: (0, 0))
    full = pl.BlockSpec(total.shape, lambda i: (0, 0))
    out = pl.BlockSpec((tokens, total.shape[1]), lambda i: (0, 0))
    return pl.pallas_call(
        functools.partial(complete_kernel, whole_tiles),
        grid=(1,),
        in_specs=[SMEM, ANY, full, w_spec, w_spec],
        out_specs=[out] * len(types),
        out_shape=[jax.ShapeDtypeStruct((tokens, total.shape[1]), t) for t in types],
        scratch_shapes=[
            pltpu.VMEM((left.shape[0], 2 * rows), jnp.bfloat16),
            pltpu.SemaphoreType.DMA((2,)),
        ],
        compiler_params=pltpu.CompilerParams(vmem_limit_bytes=24 * MIB),
        name="complete",
    )(bases, left, total, *last)


def mix_kernel(place_ref, residual_ref, gain_ref, *refs):
    parts, (mixed_ref, sent_ref) = refs[:-2], refs[-2:]
    cols = parts[0].shape[1]
    for i, part in enumerate(parts):
        here = pl.ds(pl.multiple_of(place_ref[i], cols), cols)
        there = pl.ds(pl.multiple_of(place_ref[len(parts)] + place_ref[i], cols), cols)
        mixed = residual_ref[:, there].astype(jnp.float32) + part[...].astype(jnp.float32)
        mixed_ref[:, here] = mixed
        sent_ref[:, here] = (mixed * gain_ref[:, there]).astype(jnp.bfloat16)


def mix(places, residual, gain, parts):
    shape = (residual.shape[0], residual.shape[1] // 2)
    residual = pltpu.with_memory_space_constraint(residual, pltpu.HBM)
    return pl.pallas_call(
        mix_kernel,
        in_specs=[SMEM] + [VMEM] * (2 + len(parts)),
        out_specs=[VMEM] * 2,
        out_shape=[
            jax.ShapeDtypeStruct(shape, jnp.float32),
            jax.ShapeDtypeStruct(shape, jnp.bfloat16),
        ],
        compiler_params=pltpu.CompilerParams(vmem_limit_bytes=24 * MIB),
        cost_estimate=pl.CostEstimate(flops=0, bytes_accessed=0, transcendentals=0),
        name="mix",
    )(places, residual, gain, *parts)


def finish_kernel(side_ref, *refs):
    out_ref = refs[-1]
    terms = (len(refs) - 1) // 2
    half = refs[0].shape[1]
    for h in range(2):
        total = refs[h * terms][...]
        for ref in refs[h * terms + 1 : (h + 1) * terms]:
            total = total + ref[...].astype(jnp.float32)
        at = side_ref[0] if h == 0 else 1 - side_ref[0]
        out_ref[:, pl.ds(pl.multiple_of(at * half, half), half)] = total.astype(out_ref.dtype)


def finish(side, first, second):
    tokens, half = first[0].shape
    rows = max(16, tokens // 4)
    part = pl.BlockSpec((rows, half), lambda i: (i, 0))
    return pl.pallas_call(
        finish_kernel,
        grid=(tokens // rows,),
        in_specs=[SMEM] + [part] * (len(first) + len(second)),
        out_specs=pl.BlockSpec((rows, 2 * half), lambda i: (i, 0)),
        out_shape=jax.ShapeDtypeStruct((tokens, 2 * half), jnp.bfloat16),
        compiler_params=pltpu.CompilerParams(vmem_limit_bytes=24 * MIB),
        name="finish",
    )(side, *first, *second)


def routing_kernel(cap, n_blocks, served_ref, *refs):
    sources, refs = refs[: n_blocks + 1], refs[n_blocks + 1 :]
    rows_ref, cols_ref, shares_ref, table_ref, mask, sems = refs
    tokens = mask.shape[1]
    top, lines, width = 8, table_ref.shape[1], table_ref.shape[2]
    copies = []
    for b, source in enumerate(sources):
        src = source.at[pl.ds(source.shape[0] - lines, lines)]
        if b < n_blocks - 1:
            dst = table_ref.at[b]
        else:
            at = (b - n_blocks + 1) * (width // 2)
            dst = table_ref.at[n_blocks - 1, :, pl.ds(at, width // 2)]
        copies.append(pltpu.make_async_copy(src, dst, sems.at[b]))
        copies[-1].start()
    for copy in copies:
        copy.wait()
    for b in range(n_blocks):
        parts = [
            table_ref[b, :, i * tokens : (i + 1) * tokens].astype(jnp.float32)[:top]
            for i in range(3)
        ]
        ids, share = parts[0], parts[1] + parts[2]
        at = slice(b % 2 * tokens, (b % 2 + 1) * tokens)
        for e in range(2):
            hit = ids == served_ref[e].astype(jnp.float32)
            mask[2 * b + e : 2 * b + e + 1, :] = jnp.max(
                jnp.where(hit, 1.0, 0.0), axis=0, keepdims=True
            )
            shares_ref[b // 2, e : e + 1, at] = jnp.sum(
                jnp.where(hit, share, 0.0), axis=0, keepdims=True
            )
    first = lax.broadcasted_iota(jnp.int32, (tokens, tokens), 0)
    second = lax.broadcasted_iota(jnp.int32, (tokens, tokens), 1)
    before = jnp.where(first < second, 1.0, 0.0).astype(jnp.bfloat16)
    same = jnp.where(first == second, 1.0, 0.0).astype(jnp.bfloat16)
    there = mask[...]
    rank = dot(there.astype(jnp.bfloat16), before)
    line = lax.broadcasted_iota(jnp.int32, rank.shape, 0)
    slot = jnp.where(there > 0.5, rank + jnp.where(line // 2 % 2 == 1, float(cap), 0.0), -512.0)
    columns = lax.dot_general(
        same, slot.astype(jnp.bfloat16), (((1,), (1,)), ((), ())), preferred_element_type=jnp.float32
    )
    for b in range(n_blocks):
        at = slice(b % 2 * tokens, (b % 2 + 1) * tokens)
        pair = slice(2 * b, 2 * b + 2)
        rows_ref[b // 2, :, at] = slot[pair].astype(jnp.int32)
        cols_ref[b // 2, at, :] = columns[:, pair].astype(jnp.int32)


def routing(cap, tokens, lines, served, blocks):
    blocks = [pltpu.with_memory_space_constraint(b, pltpu.HBM) for b in blocks]
    n_blocks = len(blocks) - 1
    pairs = n_blocks // 2
    rows = jax.ShapeDtypeStruct((pairs, 2, 2 * tokens), jnp.int32)
    return pl.pallas_call(
        functools.partial(routing_kernel, cap, n_blocks),
        in_specs=[SMEM] + [ANY] * len(blocks),
        out_specs=[VMEM] * 3,
        out_shape=[
            rows,
            jax.ShapeDtypeStruct((pairs, 2 * tokens, 2), jnp.int32),
            jax.ShapeDtypeStruct(rows.shape, jnp.float32),
        ],
        scratch_shapes=[
            pltpu.VMEM((n_blocks, lines, blocks[0].shape[1]), jnp.bfloat16),
            pltpu.VMEM((2 * n_blocks, tokens), jnp.float32),
            pltpu.SemaphoreType.DMA((n_blocks + 1,)),
        ],
        compiler_params=pltpu.CompilerParams(vmem_limit_bytes=16 * MIB),
        cost_estimate=pl.CostEstimate(flops=0, bytes_accessed=0, transcendentals=0),
        name="routing",
    )(served, *blocks)


def fetch_kernel(*refs):
    count = (len(refs) - 2) // 2
    token, sems = refs[-2:]
    token[...] = jnp.zeros_like(token)
    copies = [
        pltpu.make_async_copy(refs[i], refs[count + i], sems.at[i]) for i in range(count)
    ]
    for copy in copies:
        copy.start()
    for copy in copies:
        copy.wait()


def fetch(arrays):
    arrays = [pltpu.with_memory_space_constraint(a, pltpu.HBM) for a in arrays]
    *there, token = pl.pallas_call(
        fetch_kernel,
        in_specs=[ANY] * len(arrays),
        out_specs=[VMEM] * (len(arrays) + 1),
        out_shape=[pltpu.VMEM(a.shape, a.dtype) for a in arrays]
        + [jax.ShapeDtypeStruct((8, HEAD), jnp.float32)],
        scratch_shapes=[pltpu.SemaphoreType.DMA((len(arrays),))],
        compiler_params=pltpu.CompilerParams(vmem_limit_bytes=24 * MIB),
        cost_estimate=pl.CostEstimate(flops=0, bytes_accessed=0, transcendentals=0),
        name="fetch",
    )(*arrays)
    return there, token


def experts_kernel(first_pair, pairs, n_in, n_out, slots, side_ref, gain_ref, slot_rows, slot_cols, share_rows, *refs):
    x_refs = refs[:n_in]
    w_refs = refs[n_in : n_in + 6]
    out_refs = refs[n_in + 7 : n_in + 7 + n_out]
    xs, rows_in, act, scaled, x_sem = refs[n_in + 7 + n_out :]
    depth = xs.shape[1]
    pair_tokens = xs.shape[0] // pairs
    block = pair_tokens // 2
    hidden = act.shape[1]

    half = depth // 2
    starts = [pl.multiple_of(side_ref[0] * half, half), pl.multiple_of((1 - side_ref[0]) * half, half)]
    x_copies = []
    for i in range(n_in):
        dst = xs.at[pl.ds(i // 2 * block, block), pl.ds(starts[i % 2], half)]
        x_copies.append(pltpu.make_async_copy(x_refs[i], dst, x_sem.at[i]))
        x_copies[-1].start()
    for copy in x_copies:
        copy.wait()

    shares = []
    for p in range(pairs):
        row = lax.broadcasted_iota(jnp.int32, (2 * slots, pair_tokens), 0)
        first = row == slot_rows[first_pair + p, 0:1, :]
        second = row - slots == slot_rows[first_pair + p, 1:2, :]
        pick = jnp.where(first | second, 1.0, 0.0).astype(jnp.bfloat16)
        weight = jnp.where(first, share_rows[first_pair + p, 0:1, :], 0.0) + jnp.where(
            second, share_rows[first_pair + p, 1:2, :], 0.0
        )
        shares.append(jnp.sum(weight, axis=1, keepdims=True))
        step = min(1024, depth)
        for c in range(0, depth, step):
            got = dot(pick, xs[p * pair_tokens : (p + 1) * pair_tokens, c : c + step])
            got = got.astype(jnp.bfloat16)
            rows_in[0, p * slots : (p + 1) * slots, c : c + step] = got[:slots]
            rows_in[1, p * slots : (p + 1) * slots, c : c + step] = got[slots:]

    inverse = 1.0 / gain_ref[...]
    for e in range(2):
        x = rows_in[e]
        squares = 0.0
        for c in range(0, depth, HEAD):
            part = x[:, c : c + HEAD].astype(jnp.float32) * inverse[:, c : c + HEAD]
            squares = squares + part * part
        factor = lax.rsqrt(jnp.sum(squares, axis=1, keepdims=True) / depth + 1e-06)
        gate = dot(x, w_refs[3 * e][...]) * factor
        up = dot(x, w_refs[3 * e + 1][...]) * factor
        act[...] = (gate / (1.0 + jnp.exp(-gate)) * up).astype(jnp.bfloat16)
        share = jnp.concatenate([s[e * slots : (e + 1) * slots] for s in shares], axis=0)
        y = (dot(act[...], w_refs[3 * e + 2][...]) * share).astype(jnp.bfloat16)
        for p in range(pairs):
            scaled[p, e * slots : (e + 1) * slots, :] = y[p * slots : (p + 1) * slots]

    for p in range(pairs):
        lane = lax.broadcasted_iota(jnp.int32, (pair_tokens, 2 * slots), 1)
        back = lane == slot_cols[first_pair + p, :, 0:1]
        back = back | (lane - slots == slot_cols[first_pair + p, :, 1:2])
        back = jnp.where(back, 1.0, 0.0).astype(jnp.bfloat16)
        for h in range(2):
            got = dot(back, scaled[p, :, pl.ds(starts[h], half)]).astype(jnp.bfloat16)
            for b in range(2):
                out_refs[4 * p + 2 * b + h][...] = got[b * block : (b + 1) * block]


def experts(slots, first_pair, pairs, side, gain, slot_rows, slot_cols, share_rows, x_parts, weights):
    pair_tokens = slot_rows.shape[2]
    block = pair_tokens // 2
    depth, hidden = weights[0].shape
    n_in = n_out = len(x_parts)
    return pl.pallas_call(
        functools.partial(experts_kernel, first_pair, pairs, n_in, n_out, slots),
        in_specs=[SMEM] + [VMEM] * 4 + [ANY] * n_in + [VMEM] * 6 + [ANY],
        out_specs=[VMEM] * n_out,
        out_shape=[jax.ShapeDtypeStruct((block, depth // 2), jnp.bfloat16)] * n_out,
        scratch_shapes=[
            pltpu.VMEM((pairs * pair_tokens, depth), jnp.bfloat16),
            pltpu.VMEM((2, pairs * slots, depth), jnp.bfloat16),
            pltpu.VMEM((pairs * slots, hidden), jnp.bfloat16),
            pltpu.VMEM((pairs, 2 * slots, depth), jnp.bfloat16),
            pltpu.SemaphoreType.DMA((n_in,)),
        ],
        compiler_params=pltpu.CompilerParams(vmem_limit_bytes=22 * MIB),
        cost_estimate=pl.CostEstimate(
            flops=12 * pairs * slots * depth * hidden,
            bytes_accessed=12 * depth * hidden,
            transcendentals=0,
        ),
        name="experts",
    )(side, gain, slot_rows, slot_cols, share_rows, *x_parts, *weights)


def permutations(devices):
    cores, rows = 2, 2
    ring = devices // (cores * rows)

    def index(z, y, c):
        return (z % ring * rows + y % rows) * cores + c % cores

    def shift(dz, dy=0, dc=0):
        return [
            (index(z, y, c), index(z + dz + ring, y + dy, c + dc))
            for z in range(ring)
            for y in range(rows)
            for c in range(cores)
        ]

    return ring, shift


def per_device(
    residual,
    queries,
    new_keys,
    new_values,
    cache_keys,
    cache_values,
    cache_len,
    o_weight,
    norm_gain,
    expert_ids,
    gate_raw,
    w_gate,
    w_up,
    w_down,
):
    devices = lax.axis_size("wide")
    replicas = lax.axis_size("groups")
    me = lax.axis_index("wide")
    tokens, depth = residual.shape
    top = expert_ids.shape[1]
    half = depth // 2
    ring, shift = permutations(devices)
    core = me % 2
    row = me // 2 % 2
    place = me // 4
    side = lax.axis_index("groups") % 2

    def sender(*by):
        return lambda x: lax.ppermute(x, "wide", shift(*by))

    def side_sender(*by):
        pairs = [
            (g * devices + a, (g ^ 1) * devices + b)
            for g in range(replicas)
            for a, b in shift(*by)
        ]
        return lambda x: lax.ppermute(x, ("groups", "wide"), pairs)

    send_forward, send_backward = sender(1), sender(-1)
    send_across, send_core = sender(0, 1), sender(0, 0, 1)
    send_side, send_corner = side_sender(0), side_sender(0, 0, 1)
    barrier = lax.optimization_barrier

    def gather_whole(own, beside):
        same, other = [own], []
        for r in range(1, ring):
            moved, crossed = send_forward(same[-1]), send_across(same[-1])
            new = beside[r - 1](same, other) if r <= len(beside) else {}
            moved, crossed, new = barrier((moved, crossed, new))
            kept.update(new)
            same.append(moved)
            other.append(crossed)
        cut = own.shape[1] // 2
        last = [send_across(same[-1][:, :cut]), send_forward(other[-1][:, cut:])]
        for step in beside[ring - 1 :]:
            last, new = barrier((last, step(same, other)))
            kept.update(new)
        return same, other, last

    def gather_halves(own, beside, held):
        same, other = [list(own)], []
        for r in range(1, ring):
            moved = [send_forward(h) for h in same[-1]]
            crossed = [send_across(h) for h in same[-1]]
            if r == 1:
                same[0] = list(held)
            new = beside[r - 1](same, other) if r <= len(beside) else {}
            moved[0], crossed[0] = barrier((moved[0], crossed[0]))
            moved[1], crossed[1], new = barrier((moved[1], crossed[1], new))
            kept.update(new)
            same.append(moved)
            other.append(crossed)
        last = [send_across(same[-1][0]), send_forward(other[-1][1])]
        for step in beside[ring - 1 :]:
            last, new = barrier((last, step(same, other)))
            kept.update(new)
        other.append(last)
        return same, other

    kept = {}

    def nothing(same, other):
        return {}

    cols = depth // 4
    quarter = 2 * side + core
    keep = lax.dynamic_slice_in_dim(o_weight, quarter * cols, cols, 1)
    give = lax.dynamic_slice_in_dim(o_weight, (quarter ^ 1) * cols, cols, 1)
    shares = gate_raw / jnp.sum(gate_raw, axis=-1, keepdims=True)
    high = shares.astype(jnp.bfloat16)
    low = (shares - high.astype(jnp.float32)).astype(jnp.bfloat16)
    table = jnp.concatenate([expert_ids.astype(jnp.bfloat16).T, high.T, low.T], axis=1)
    lines = 16
    table = jnp.pad(table, ((0, lines - top), (0, cols - 3 * tokens)))
    own_block = jnp.concatenate([keep, send_core(give), table], axis=0)
    length = lax.dynamic_slice_in_dim(cache_len, me, 1, 0)
    mine = [w_gate[0], w_up[0], w_down[0]]
    length, own_block, mine = barrier((length, own_block, mine))
    operands = (queries, new_keys, new_values, cache_keys[0], cache_values[0])

    late = {}

    def attend_first(same, other):
        return {"a0": attention(0, 2, length, *operands), "w0": send_core(mine[0])}

    def attend_second(same, other):
        begin, kept["a0"] = barrier((length, kept["a0"]))
        return {
            "a1": attention(1, 2, begin, *operands),
            "side0": send_side(kept["a0"]),
            "w1": send_core(mine[1]),
        }

    def swap_first(same, other):
        late["side1"] = send_side(kept["a1"])
        return {"core0": send_core(kept["a0"]), "w2": send_core(mine[2])}

    offsets = jnp.arange(ring, dtype=jnp.int32)
    rings = (place - offsets) % ring
    first_of = jnp.concatenate([rings * 2 + row, rings * 2 + 1 - row]) * 2
    bases = jnp.stack([first_of + core, first_of + 1 - core], axis=1).reshape(-1)
    bases = bases * o_weight.shape[0]

    def project(same, other):
        kept["core1"] = send_core(kept["a1"])
        kept["corner0"] = send_core(kept["side0"])
        kept["corner1"] = send_core(late["side1"])
        kept.update(late)
        pieces = [kept[name + str(g)] for name in ("a", "core", "side", "corner") for g in range(2)]
        left, total = projection(bases, pieces, 4, same + other)
        return {"left": left, "sum": total}

    w_same, w_other, w_last = gather_whole(
        own_block, [attend_first, attend_second, swap_first] + [nothing] * (ring - 4) + [project]
    )
    types = [jnp.float32, jnp.float32, jnp.bfloat16, jnp.bfloat16]
    own_part, core_part, side_part, corner_part = complete(
        bases[-2:], o_weight.shape[0], kept["left"], kept["sum"], w_last, types
    )

    gain = norm_gain.reshape(1, -1)
    near = [own_part, send_core(core_part)]
    far = [send_side(side_part), send_corner(corner_part)]
    here = [core * cols, (1 - core) * cols]
    mixed_near, x_near = mix(jnp.stack(here + [side * half]).astype(jnp.int32), residual, gain, near)
    far_places = jnp.stack(here + [(1 - side) * half]).astype(jnp.int32)
    cap = tokens * top // devices + max(2, tokens * top // (8 * devices))
    slots = -(-2 * cap // 16) * 16
    served = jnp.stack([me, me ^ 1])
    w_blocks, x_near_later = barrier((w_same + w_other + w_last, x_near))
    order = []
    for r in range(0, ring, 2):
        order += w_blocks[r : r + 2] + w_blocks[ring + r : ring + r + 2]
    order.append(w_blocks[-1])
    tables = routing(cap, tokens, lines, served, order)
    far, tables = barrier((far, tables))
    mixed_far, x_far = mix(far_places, residual, gain, far)
    side_word = side.astype(jnp.int32).reshape(1)

    def load_weights(same, other):
        arrays = mine + [kept["w0"], kept["w1"], kept["w2"]]
        arrays, kept["tables"], same[1][1] = barrier((arrays, tables, same[1][1]))
        weights, token = fetch(arrays)
        beside_weights.extend(weights)
        return {"token": token}

    beside_weights = []

    def serve(first, count, blocks):
        halves = [h for block in blocks for h in block]
        weights = beside_weights + [kept["token"]]
        outs = experts(slots, first, count, side_word, gain, *kept["tables"], halves, weights)
        return [outs[i : i + 2] for i in range(0, len(outs), 2)]

    def serve_same(r):
        def step(same, other):
            p0, p1 = serve(r, 1, same[r : r + 2])
            return {("p", r): p0, ("p", r + 1): p1}

        return step

    def serve_other(r):
        def step(same, other):
            q0, q1 = serve(r + 1, 1, other[r : r + 2])
            return {("q", r): q0, ("q", r + 1): q1}

        return step

    def serve_two(same, other):
        p0, p1 = serve(ring - 2, 1, same[-2:])
        return {("p", ring - 2): p0, ("p", ring - 1): p1}

    beside = [nothing, load_weights, serve_other(0)]
    for r in range(2, ring - 2, 2):
        beside += [serve_same(r), serve_other(r)]
    beside.append(serve_two)
    x_same, x_other = gather_halves([x_near, x_far], beside, [x_near_later, x_far])
    p = [None, None] + [kept["p", r] for r in range(2, ring)]
    q = [kept["q", r] for r in range(ring - 2)]
    q += serve(ring - 1, 1, x_other[-2:])

    def add(*terms):
        return sum(t.astype(jnp.float32) for t in terms).astype(jnp.bfloat16)

    r = ring - 1
    came = [None, send_backward(p[r][1])]
    extra = send_backward(q[r][1])
    crossed = [send_across(q[r][0]), None]
    later = [send_across(q[r - 1][0]), None]
    p[0], p[1] = serve(0, 1, x_same[:2])
    crossed[1] = send_across(add(q[r - 1][1], extra))
    came[0] = send_backward(add(p[r][0], crossed[0]))
    crossed[0] = later[0]
    for r in range(ring - 2, 0, -1):
        moving = [None, None]
        for h in (1, 0):
            total = add(p[r][h], came[h], crossed[h])
            total, behind = barrier((total, q[r - 1][h]))
            came[h], crossed[h] = send_backward(total), send_across(behind)
    mixed = [mixed_near, mixed_far]
    return finish(side_word, *[[mixed[h], p[0][h], came[h], crossed[h]] for h in range(2)])


def solution(mesh):
    placed = (
        P(("groups", "wide"), None),
        P(("groups", "wide"), None),
        P(("groups", "wide"), None),
        P(("groups", "wide"), None),
        P(("groups", "wide"), None, None),
        P(("groups", "wide"), None, None),
        P("groups"),
        P("wide", None),
        P(),
        P(("groups", "wide"), None),
        P(("groups", "wide"), None),
        P("wide", None, None),
        P("wide", None, None),
        P("wide", None, None),
    )
    return jax.shard_map(
        per_device,
        mesh=mesh,
        in_specs=placed,
        out_specs=P(("groups", "wide"), None),
        check_vma=False,
    )
```

```python
import functools

import jax
import jax.numpy as jnp
from jax import lax
from jax.experimental import pallas as pl
from jax.experimental.pallas import tpu as pltpu
from jax.sharding import PartitionSpec as P

HEAD = 128
KEY_BLOCK = 1024
LOG2E = 1.4426950408889634
NEG = -1e30
MIB = 1 << 20

VMEM = pl.BlockSpec(memory_space=pltpu.VMEM)
SMEM = pl.BlockSpec(memory_space=pltpu.SMEM)
ANY = pl.BlockSpec(memory_space=pl.ANY)


def place_of(ring):
    me = lax.axis_index("wide")
    return me // 4 % ring, me // 2 % 2, me % 2


def dot(a, b):
    return jnp.dot(a, b, preferred_element_type=jnp.float32)


def attention_kernel(
    part, len_ref, q_ref, nk_ref, nv_ref, k_any, v_any, o_ref, q_all, scores, top, acc, total, k_ref, v_ref, sems
):
    tokens = q_ref.shape[0]
    heads = q_ref.shape[1] // HEAD
    cache = k_any.shape[0]
    length = len_ref[lax.axis_index("wide")]
    blocks = (length + KEY_BLOCK - 1) // KEY_BLOCK
    scale = jnp.float32(HEAD**-0.5 * LOG2E)
    at = pl.ds(part * HEAD, HEAD)
    copies = [
        pltpu.make_async_copy(any_ref.at[:, at], ref, sems.at[i])
        for i, (any_ref, ref) in enumerate(((k_any, k_ref), (v_any, v_ref)))
    ]
    for copy in copies:
        copy.start()

    for h in range(heads):
        q_all[h * tokens : (h + 1) * tokens, :] = q_ref[:, h * HEAD : (h + 1) * HEAD]

    def scores_of(k):
        return lax.dot_general(
            q_all[...], k, (((1,), (1,)), ((), ())), preferred_element_type=jnp.float32
        )

    def fold(x, op):
        parts = [x[:, i : i + HEAD] for i in range(0, x.shape[1], HEAD)]
        while len(parts) > 1:
            parts = [op(*parts[i : i + 2]) if i + 1 < len(parts) else parts[i] for i in range(0, len(parts), 2)]
        return parts[0]

    s = scores_of(nk_ref[...])
    row = lax.broadcasted_iota(jnp.int32, s.shape, 0) % tokens
    col = lax.broadcasted_iota(jnp.int32, s.shape, 1)
    s = jnp.where(col <= row, s, NEG)
    scores[:, cache:] = s
    top[...] = fold(s, jnp.maximum)

    def score(i, carry):
        at = pl.ds(pl.multiple_of(i * KEY_BLOCK, KEY_BLOCK), KEY_BLOCK)
        s = scores_of(k_ref[at, :])
        pos = lax.broadcasted_iota(jnp.int32, s.shape, 1)
        s = jnp.where(pos < length - i * KEY_BLOCK, s, NEG)
        scores[:, at] = s
        top[...] = jnp.maximum(top[...], fold(s, jnp.maximum))
        return carry

    copies[0].wait()
    lax.fori_loop(0, blocks, score, 0)
    best = jnp.max(top[...], axis=1, keepdims=True) * scale
    top[...] = jnp.broadcast_to(best, top.shape)

    def weigh(s):
        shift = jnp.concatenate([top[...]] * (s.shape[1] // HEAD), axis=1)
        return jnp.exp2(s * scale - shift)

    w = weigh(scores[:, cache:])
    total[...] = fold(w, jnp.add)
    acc[...] = dot(w.astype(jnp.bfloat16), nv_ref[...])

    def add_block(i, carry):
        at = pl.ds(pl.multiple_of(i * KEY_BLOCK, KEY_BLOCK), KEY_BLOCK)
        w = weigh(scores[:, at])
        total[...] += fold(w, jnp.add)
        acc[...] += dot(w.astype(jnp.bfloat16), v_ref[at, :])
        return carry

    copies[1].wait()
    lax.fori_loop(0, blocks, add_block, 0)
    out = (acc[...] / jnp.sum(total[...], axis=1, keepdims=True)).astype(jnp.bfloat16)
    for h in range(heads):
        o_ref[:, h * HEAD : (h + 1) * HEAD] = out[h * tokens : (h + 1) * tokens, :]


def attention(part, parts, length, queries, new_keys, new_values, keys, values):
    tokens, width = queries.shape
    kv_heads = new_keys.shape[1] // HEAD
    g = part * kv_heads // parts
    group = width // parts
    cache = keys.shape[0]
    rows = group // HEAD * tokens
    keys, values = [pltpu.with_memory_space_constraint(a, pltpu.HBM) for a in (keys, values)]
    return pl.pallas_call(
        functools.partial(attention_kernel, g),
        grid=(1,),
        in_specs=[
            SMEM,
            pl.BlockSpec((tokens, group), lambda i: (0, part)),
            pl.BlockSpec((tokens, HEAD), lambda i: (0, g)),
            pl.BlockSpec((tokens, HEAD), lambda i: (0, g)),
            ANY,
            ANY,
        ],
        out_specs=pl.BlockSpec((tokens, group), lambda i: (0, 0)),
        out_shape=jax.ShapeDtypeStruct((tokens, group), jnp.bfloat16),
        scratch_shapes=[
            pltpu.VMEM((rows, HEAD), jnp.bfloat16),
            pltpu.VMEM((rows, cache + tokens), jnp.float32),
            pltpu.VMEM((rows, HEAD), jnp.float32),
            pltpu.VMEM((rows, HEAD), jnp.float32),
            pltpu.VMEM((rows, HEAD), jnp.float32),
            pltpu.VMEM((cache, HEAD), jnp.bfloat16),
            pltpu.VMEM((cache, HEAD), jnp.bfloat16),
            pltpu.SemaphoreType.DMA((2,)),
        ],
        compiler_params=pltpu.CompilerParams(vmem_limit_bytes=58 * MIB),
        cost_estimate=pl.CostEstimate(
            flops=20 * tokens * group * cache,
            bytes_accessed=4 * cache * HEAD,
            transcendentals=tokens * group // HEAD * cache,
        ),
        name="attention",
    )(length, queries, new_keys, new_values, keys, values)


def projection_kernel(n_pieces, n_blocks, *refs):
    pieces, w_refs = refs[:n_pieces], refs[n_pieces : n_pieces + n_blocks - 1]
    sum_out, left_out, left, weight, sems = refs[n_pieces + n_blocks - 1 :]
    tokens, group = pieces[0].shape
    rows = weight.shape[0] // n_blocks // 2
    each = left.shape[1] // group
    ring = n_blocks // 2
    place, row, core = place_of(ring)
    copies = []

    def first_row(b, part):
        z = lax.rem(place + ring - b % ring, ring)
        y = row if b < ring else 1 - row
        c = core if part == 0 else 1 - core
        return pl.multiple_of(((z * 2 + y) * 2 + c) * rows, rows)

    def begin(src, dst):
        copies.append(pltpu.make_async_copy(src, dst, sems.at[len(copies)]))
        copies[-1].start()

    for b in range(n_blocks - 1):
        for part in range(2):
            at = first_row(b, part)
            begin(w_refs[b].at[pl.ds(part * rows, rows)], weight.at[pl.ds(at, rows)])
    for i, piece in enumerate(pieces):
        dst = left.at[pl.ds(i // each * tokens, tokens), pl.ds(i % each * group, group)]
        begin(piece, dst)
    for part in range(2):
        at = first_row(n_blocks - 1, part)
        weight[pl.ds(at, rows), :] = jnp.zeros((rows, weight.shape[1]), weight.dtype)
    for copy in copies:
        copy.wait()
    sum_out[...] = dot(left[...], weight[...])
    if left_out.shape == left.shape:
        left_out[...] = left[...]
    else:
        for part in range(2):
            at = first_row(n_blocks - 1, part)
            left_out[:, part * rows : (part + 1) * rows] = left[:, pl.ds(at, rows)]


def projection(rows, pieces, count, blocks):
    tokens, group = pieces[0].shape
    width = len(pieces) // count * group
    n_blocks = len(blocks) + 1
    cols = blocks[0].shape[1]
    whole_tiles = rows % HEAD == 0
    pieces, blocks = [
        [pltpu.with_memory_space_constraint(a, pltpu.HBM) for a in arrays] for arrays in (pieces, blocks)
    ]
    total, left = pl.pallas_call(
        functools.partial(projection_kernel, len(pieces), n_blocks),
        in_specs=[ANY] * (len(pieces) + len(blocks)),
        out_specs=[VMEM] * 2,
        out_shape=[
            jax.ShapeDtypeStruct((count * tokens, cols), jnp.float32),
            jax.ShapeDtypeStruct((count * tokens, 2 * rows), jnp.bfloat16)
            if whole_tiles
            else jax.ShapeDtypeStruct((count * tokens, width), jnp.bfloat16),
        ],
        scratch_shapes=[
            pltpu.VMEM((count * tokens, width), jnp.bfloat16),
            pltpu.VMEM((width, cols), jnp.bfloat16),
            pltpu.SemaphoreType.DMA((2 * n_blocks - 2 + len(pieces),)),
        ],
        compiler_params=pltpu.CompilerParams(vmem_limit_bytes=20 * MIB),
        cost_estimate=pl.CostEstimate(
            flops=8 * tokens * width * cols, bytes_accessed=2 * width * cols, transcendentals=0
        ),
        name="projection",
    )(*pieces, *blocks)
    if not whole_tiles:
        ring = n_blocks // 2
        place, row, core = place_of(ring)
        source = ((place + 1) % ring * 2 + 1 - row) * 2
        parts = [
            lax.dynamic_slice_in_dim(left, (source + c) * rows, rows, 1) for c in (core, 1 - core)
        ]
        left = jnp.concatenate(parts, axis=1)
    return total, left


def complete_kernel(sum_ref, left_ref, first_ref, second_ref, *outs):
    tokens = outs[0].shape[0]
    half, rows = first_ref.shape[1], left_ref.shape[1]
    for h, w_ref in enumerate((first_ref, second_ref)):
        cols = slice(h * half, (h + 1) * half)
        whole = sum_ref[:, cols] + dot(left_ref[...], w_ref[:rows, :])
        for i, out in enumerate(outs):
            out[:, cols] = whole[i * tokens : (i + 1) * tokens].astype(out.dtype)


def complete(total, left, last, types):
    tokens = left.shape[0] // len(types)
    return pl.pallas_call(
        complete_kernel,
        in_specs=[VMEM] * 4,
        out_specs=[VMEM] * len(types),
        out_shape=[jax.ShapeDtypeStruct((tokens, total.shape[1]), t) for t in types],
        compiler_params=pltpu.CompilerParams(vmem_limit_bytes=16 * MIB),
        name="complete",
    )(total, left, *last)


def mix_kernel(far, residual_ref, gain_ref, *refs):
    parts, (mixed_ref, sent_ref) = refs[:-2], refs[-2:]
    cols = parts[0].shape[1]
    for i, part in enumerate(parts):
        core = lax.axis_index("wide") % 2
        side = lax.axis_index("groups") % 2
        at = (1 - core if i else core) * cols
        base = (1 - side if far else side) * 2 * cols
        here = pl.ds(pl.multiple_of(at, cols), cols)
        there = pl.ds(pl.multiple_of(base + at, cols), cols)
        mixed = residual_ref[:, there].astype(jnp.float32) + part[...].astype(jnp.float32)
        mixed_ref[:, here] = mixed
        sent_ref[:, here] = (mixed * gain_ref[:, there]).astype(jnp.bfloat16)


def mix(far, residual, gain, parts):
    shape = (residual.shape[0], residual.shape[1] // 2)
    residual = pltpu.with_memory_space_constraint(residual, pltpu.HBM)
    return pl.pallas_call(
        functools.partial(mix_kernel, far),
        in_specs=[VMEM] * (2 + len(parts)),
        out_specs=[VMEM] * 2,
        out_shape=[
            jax.ShapeDtypeStruct(shape, jnp.float32),
            jax.ShapeDtypeStruct(shape, jnp.bfloat16),
        ],
        compiler_params=pltpu.CompilerParams(vmem_limit_bytes=24 * MIB),
        cost_estimate=pl.CostEstimate(flops=0, bytes_accessed=0, transcendentals=0),
        name="mix",
    )(residual, gain, *parts)


def finish_kernel(*refs):
    out_ref = refs[-1]
    terms = (len(refs) - 1) // 2
    half = refs[0].shape[1]
    side = lax.axis_index("groups") % 2
    for h in range(2):
        total = refs[h * terms][...]
        for ref in refs[h * terms + 1 : (h + 1) * terms]:
            total = total + ref[...].astype(jnp.float32)
        at = side if h == 0 else 1 - side
        out_ref[:, pl.ds(pl.multiple_of(at * half, half), half)] = total.astype(out_ref.dtype)


def finish(first, second):
    tokens, half = first[0].shape
    rows = max(16, tokens // 4)
    part = pl.BlockSpec((rows, half), lambda i: (i, 0))
    return pl.pallas_call(
        finish_kernel,
        grid=(tokens // rows,),
        in_specs=[part] * (len(first) + len(second)),
        out_specs=pl.BlockSpec((rows, 2 * half), lambda i: (i, 0)),
        out_shape=jax.ShapeDtypeStruct((tokens, 2 * half), jnp.bfloat16),
        compiler_params=pltpu.CompilerParams(vmem_limit_bytes=24 * MIB),
        name="finish",
    )(*first, *second)


def routing_kernel(cap, n_blocks, *refs):
    sources, refs = refs[: n_blocks + 1], refs[n_blocks + 1 :]
    rows_ref, cols_ref, shares_ref, table_ref, mask, sems = refs
    tokens = mask.shape[1]
    top, lines, width = 8, table_ref.shape[1], table_ref.shape[2]
    copies = []
    for b, source in enumerate(sources):
        src = source.at[pl.ds(source.shape[0] - lines, lines)]
        if b < n_blocks - 1:
            dst = table_ref.at[b]
        else:
            at = (b - n_blocks + 1) * (width // 2)
            dst = table_ref.at[n_blocks - 1, :, pl.ds(at, width // 2)]
        copies.append(pltpu.make_async_copy(src, dst, sems.at[b]))
        copies[-1].start()
    for copy in copies:
        copy.wait()
    me = lax.axis_index("wide")
    served = [me.astype(jnp.float32), (me + 1 - 2 * (me % 2)).astype(jnp.float32)]
    for b in range(n_blocks):
        parts = [
            table_ref[b, :, i * tokens : (i + 1) * tokens].astype(jnp.float32)[:top]
            for i in range(3)
        ]
        ids, score = parts[0], parts[1] + parts[2]
        share = score / jnp.sum(score, axis=0, keepdims=True)
        at = slice(b % 2 * tokens, (b % 2 + 1) * tokens)
        for e in range(2):
            hit = ids == served[e]
            mask[2 * b + e : 2 * b + e + 1, :] = jnp.max(
                jnp.where(hit, 1.0, 0.0), axis=0, keepdims=True
            )
            shares_ref[b // 2, e : e + 1, at] = jnp.sum(
                jnp.where(hit, share, 0.0), axis=0, keepdims=True
            )
    first = lax.broadcasted_iota(jnp.int32, (tokens, tokens), 0)
    second = lax.broadcasted_iota(jnp.int32, (tokens, tokens), 1)
    before = jnp.where(first < second, 1.0, 0.0).astype(jnp.bfloat16)
    same = jnp.where(first == second, 1.0, 0.0).astype(jnp.bfloat16)
    there = mask[...]
    rank = dot(there.astype(jnp.bfloat16), before)
    line = lax.broadcasted_iota(jnp.int32, rank.shape, 0)
    slot = jnp.where(there > 0.5, rank + jnp.where(line // 2 % 2 == 1, float(cap), 0.0), -512.0)
    columns = lax.dot_general(
        same, slot.astype(jnp.bfloat16), (((1,), (1,)), ((), ())), preferred_element_type=jnp.float32
    )
    for b in range(n_blocks):
        at = slice(b % 2 * tokens, (b % 2 + 1) * tokens)
        pair = slice(2 * b, 2 * b + 2)
        rows_ref[b // 2, :, at] = slot[pair].astype(jnp.int32)
        cols_ref[b // 2, at, :] = columns[:, pair].astype(jnp.int32)


def routing(cap, tokens, lines, blocks):
    blocks = [pltpu.with_memory_space_constraint(b, pltpu.HBM) for b in blocks]
    n_blocks = len(blocks) - 1
    pairs = n_blocks // 2
    rows = jax.ShapeDtypeStruct((pairs, 2, 2 * tokens), jnp.int32)
    return pl.pallas_call(
        functools.partial(routing_kernel, cap, n_blocks),
        in_specs=[ANY] * len(blocks),
        out_specs=[VMEM] * 3,
        out_shape=[
            rows,
            jax.ShapeDtypeStruct((pairs, 2 * tokens, 2), jnp.int32),
            jax.ShapeDtypeStruct(rows.shape, jnp.float32),
        ],
        scratch_shapes=[
            pltpu.VMEM((n_blocks, lines, blocks[0].shape[1]), jnp.bfloat16),
            pltpu.VMEM((2 * n_blocks, tokens), jnp.float32),
            pltpu.SemaphoreType.DMA((n_blocks + 1,)),
        ],
        compiler_params=pltpu.CompilerParams(vmem_limit_bytes=16 * MIB),
        cost_estimate=pl.CostEstimate(flops=0, bytes_accessed=0, transcendentals=0),
        name="routing",
    )(*blocks)


def fetch_kernel(*refs):
    count = (len(refs) - 2) // 2
    token, sems = refs[-2:]
    token[...] = jnp.zeros_like(token)
    copies = [
        pltpu.make_async_copy(refs[i], refs[count + i], sems.at[i]) for i in range(count)
    ]
    for copy in copies:
        copy.start()
    for copy in copies:
        copy.wait()


def fetch(arrays):
    arrays = [pltpu.with_memory_space_constraint(a, pltpu.HBM) for a in arrays]
    *there, token = pl.pallas_call(
        fetch_kernel,
        in_specs=[ANY] * len(arrays),
        out_specs=[VMEM] * (len(arrays) + 1),
        out_shape=[pltpu.VMEM(a.shape, a.dtype) for a in arrays]
        + [jax.ShapeDtypeStruct((8, HEAD), jnp.float32)],
        scratch_shapes=[pltpu.SemaphoreType.DMA((len(arrays),))],
        compiler_params=pltpu.CompilerParams(vmem_limit_bytes=24 * MIB),
        cost_estimate=pl.CostEstimate(flops=0, bytes_accessed=0, transcendentals=0),
        name="fetch",
    )(*arrays)
    return there, token


def experts_kernel(first_pair, pairs, n_in, n_out, slots, gain_ref, slot_rows, slot_cols, share_rows, *refs):
    x_refs = refs[:n_in]
    w_refs = refs[n_in : n_in + 6]
    out_refs = refs[n_in + 8 : n_in + 8 + n_out]
    xs, rows_in, act, scaled, x_sem = refs[n_in + 8 + n_out :]
    depth = xs.shape[1]
    pair_tokens = xs.shape[0] // pairs
    block = pair_tokens // 2
    hidden = act.shape[1]

    half = depth // 2
    side = lax.axis_index("groups") % 2
    starts = [pl.multiple_of(side * half, half), pl.multiple_of((1 - side) * half, half)]
    x_copies = []
    for i in range(n_in):
        dst = xs.at[pl.ds(i // 2 * block, block), pl.ds(starts[i % 2], half)]
        x_copies.append(pltpu.make_async_copy(x_refs[i], dst, x_sem.at[i]))
        x_copies[-1].start()
    for copy in x_copies:
        copy.wait()

    shares = []
    for p in range(pairs):
        row = lax.broadcasted_iota(jnp.int32, (2 * slots, pair_tokens), 0)
        first = row == slot_rows[first_pair + p, 0:1, :]
        second = row - slots == slot_rows[first_pair + p, 1:2, :]
        pick = jnp.where(first | second, 1.0, 0.0).astype(jnp.bfloat16)
        weight = jnp.where(first, share_rows[first_pair + p, 0:1, :], 0.0) + jnp.where(
            second, share_rows[first_pair + p, 1:2, :], 0.0
        )
        shares.append(jnp.sum(weight, axis=1, keepdims=True))
        step = min(1024, depth)
        for c in range(0, depth, step):
            got = dot(pick, xs[p * pair_tokens : (p + 1) * pair_tokens, c : c + step])
            got = got.astype(jnp.bfloat16)
            rows_in[0, p * slots : (p + 1) * slots, c : c + step] = got[:slots]
            rows_in[1, p * slots : (p + 1) * slots, c : c + step] = got[slots:]

    inverse = 1.0 / gain_ref[...]
    for e in range(2):
        x = rows_in[e]
        squares = 0.0
        for c in range(0, depth, HEAD):
            part = x[:, c : c + HEAD].astype(jnp.float32) * inverse[:, c : c + HEAD]
            squares = squares + part * part
        factor = lax.rsqrt(jnp.sum(squares, axis=1, keepdims=True) / depth + 1e-06)
        gate = dot(x, w_refs[3 * e][...]) * factor
        up = dot(x, w_refs[3 * e + 1][...]) * factor
        act[...] = (gate / (1.0 + jnp.exp(-gate)) * up).astype(jnp.bfloat16)
        share = jnp.concatenate([s[e * slots : (e + 1) * slots] for s in shares], axis=0)
        y = (dot(act[...], w_refs[3 * e + 2][...]) * share).astype(jnp.bfloat16)
        for p in range(pairs):
            scaled[p, e * slots : (e + 1) * slots, :] = y[p * slots : (p + 1) * slots]

    for p in range(pairs):
        lane = lax.broadcasted_iota(jnp.int32, (pair_tokens, 2 * slots), 1)
        back = lane == slot_cols[first_pair + p, :, 0:1]
        back = back | (lane - slots == slot_cols[first_pair + p, :, 1:2])
        back = jnp.where(back, 1.0, 0.0).astype(jnp.bfloat16)
        for h in range(2):
            got = dot(back, scaled[p, :, pl.ds(starts[h], half)]).astype(jnp.bfloat16)
            for b in range(2):
                out_refs[4 * p + 2 * b + h][...] = got[b * block : (b + 1) * block]


def experts(slots, first_pair, pairs, gain, slot_rows, slot_cols, share_rows, x_parts, weights):
    pair_tokens = slot_rows.shape[2]
    block = pair_tokens // 2
    depth, hidden = weights[0].shape
    n_in = n_out = len(x_parts)
    return pl.pallas_call(
        functools.partial(experts_kernel, first_pair, pairs, n_in, n_out, slots),
        in_specs=[VMEM] * 4 + [ANY] * n_in + [VMEM] * 6 + [ANY] * 2,
        out_specs=[VMEM] * n_out,
        out_shape=[jax.ShapeDtypeStruct((block, depth // 2), jnp.bfloat16)] * n_out,
        scratch_shapes=[
            pltpu.VMEM((pairs * pair_tokens, depth), jnp.bfloat16),
            pltpu.VMEM((2, pairs * slots, depth), jnp.bfloat16),
            pltpu.VMEM((pairs * slots, hidden), jnp.bfloat16),
            pltpu.VMEM((pairs, 2 * slots, depth), jnp.bfloat16),
            pltpu.SemaphoreType.DMA((n_in,)),
        ],
        compiler_params=pltpu.CompilerParams(vmem_limit_bytes=22 * MIB),
        cost_estimate=pl.CostEstimate(
            flops=12 * pairs * slots * depth * hidden,
            bytes_accessed=12 * depth * hidden,
            transcendentals=0,
        ),
        name="experts",
    )(gain, slot_rows, slot_cols, share_rows, *x_parts, *weights)


def permutations(devices):
    cores, rows = 2, 2
    ring = devices // (cores * rows)

    def index(z, y, c):
        return (z % ring * rows + y % rows) * cores + c % cores

    def shift(dz, dy=0, dc=0):
        return [
            (index(z, y, c), index(z + dz + ring, y + dy, c + dc))
            for z in range(ring)
            for y in range(rows)
            for c in range(cores)
        ]

    return ring, shift


def per_device(
    residual,
    queries,
    new_keys,
    new_values,
    cache_keys,
    cache_values,
    cache_len,
    o_weight,
    norm_gain,
    expert_ids,
    gate_raw,
    w_gate,
    w_up,
    w_down,
):
    devices = lax.axis_size("wide")
    replicas = lax.axis_size("groups")
    me = lax.axis_index("wide")
    tokens, depth = residual.shape
    top = expert_ids.shape[1]
    half = depth // 2
    ring, shift = permutations(devices)
    core = me % 2
    side = lax.axis_index("groups") % 2

    def sender(*by):
        return lambda x: lax.ppermute(x, "wide", shift(*by))

    def side_sender(*by):
        pairs = [
            (g * devices + a, (g ^ 1) * devices + b)
            for g in range(replicas)
            for a, b in shift(*by)
        ]
        return lambda x: lax.ppermute(x, ("groups", "wide"), pairs)

    send_forward, send_backward = sender(1), sender(-1)
    send_across, send_core = sender(0, 1), sender(0, 0, 1)
    send_side, send_corner = side_sender(0), side_sender(0, 0, 1)
    barrier = lax.optimization_barrier

    def gather_whole(own, beside):
        same, other = [own], []
        for r in range(1, ring):
            moved, crossed = send_forward(same[-1]), send_across(same[-1])
            new = beside[r - 1](same, other) if r <= len(beside) else {}
            moved, crossed, new = barrier((moved, crossed, new))
            kept.update(new)
            same.append(moved)
            other.append(crossed)
        cut = own.shape[1] // 2
        last = [send_across(same[-1][:, :cut]), send_forward(other[-1][:, cut:])]
        for step in beside[ring - 1 :]:
            last, new = barrier((last, step(same, other)))
            kept.update(new)
        return same, other, last

    def gather_halves(own, beside, held):
        same, other = [list(own)], []
        for r in range(1, ring):
            moved = [send_forward(h) for h in same[-1]]
            crossed = [send_across(h) for h in same[-1]]
            if r == 1:
                same[0] = list(held)
            new = beside[r - 1](same, other) if r <= len(beside) else {}
            moved[0], crossed[0] = barrier((moved[0], crossed[0]))
            moved[1], crossed[1], new = barrier((moved[1], crossed[1], new))
            kept.update(new)
            same.append(moved)
            other.append(crossed)
        last = [send_forward(other[-1][0]), send_across(same[-1][1])]
        for step in beside[ring - 1 :]:
            last, new = barrier((last, step(same, other)))
            kept.update(new)
        other.append(last)
        return same, other

    kept = {}

    def nothing(same, other):
        return {}

    cols = depth // 4
    quarter = 2 * side + core
    keep = lax.dynamic_slice_in_dim(o_weight, quarter * cols, cols, 1)
    give = lax.dynamic_slice_in_dim(o_weight, (quarter ^ 1) * cols, cols, 1)
    high = gate_raw.astype(jnp.bfloat16)
    low = (gate_raw - high.astype(jnp.float32)).astype(jnp.bfloat16)
    table = jnp.concatenate([expert_ids.astype(jnp.bfloat16).T, high.T, low.T], axis=1)
    lines = 16
    table = jnp.pad(table, ((0, lines - top), (0, cols - 3 * tokens)))
    own_block = jnp.concatenate([keep, send_core(give), table], axis=0)
    length = cache_len
    mine = [w_gate[0], w_up[0], w_down[0]]
    length, own_block, mine = barrier((length, own_block, mine))
    operands = (queries, new_keys, new_values, cache_keys[0], cache_values[0])

    late = {}
    beside_weights = []

    def attend_first(same, other):
        return {"a0": attention(0, 2, length, *operands), "w0": send_core(mine[0])}

    def attend_second(same, other):
        begin, kept["a0"] = barrier((length, kept["a0"]))
        return {
            "a1": attention(1, 2, begin, *operands),
            "side0": send_side(kept["a0"]),
            "w1": send_core(mine[1]),
        }

    def swap_first(same, other):
        late["side1"] = send_side(kept["a1"])
        return {"core0": send_core(kept["a0"]), "w2": send_core(mine[2])}

    def project(same, other):
        kept["core1"] = send_core(kept["a1"])
        kept["corner0"] = send_core(kept["side0"])
        kept["corner1"] = send_core(late["side1"])
        kept.update(late)
        pieces = [kept[name + str(g)] for name in ("a", "core", "side", "corner") for g in range(2)]
        return {"sum": projection(o_weight.shape[0], pieces, 4, same + other)}

    w_same, w_other, w_last = gather_whole(
        own_block, [attend_first, attend_second, swap_first] + [nothing] * (ring - 4) + [project]
    )
    types = [jnp.float32, jnp.float32, jnp.bfloat16, jnp.bfloat16]
    own_part, core_part, side_part, corner_part = complete(
        *kept["sum"], w_last, types
    )

    gain = norm_gain.reshape(1, -1)
    near = [own_part, send_core(core_part)]
    far = [send_side(side_part), send_corner(corner_part)]
    mixed_near, x_near = mix(False, residual, gain, near)
    cap = tokens * top // devices + max(2, tokens * top // (8 * devices))
    slots = -(-2 * cap // 16) * 16
    w_blocks, x_near_later = barrier((w_same + w_other + w_last, x_near))
    order = []
    for r in range(0, ring - 2, 2):
        order += w_blocks[r : r + 2] + w_blocks[ring + r : ring + r + 2]
    order += [w_blocks[ring - 2], w_blocks[-3], w_blocks[ring - 1]] + w_blocks[-2:]
    tables = routing(cap, tokens, lines, order)
    far, tables = barrier((far, tables))
    mixed_far, x_far = mix(True, residual, gain, far)

    def load_mine(same, other):
        arrays, kept["tables"], same[0][1] = barrier((mine, tables, same[0][1]))
        weights, token = fetch(arrays)
        beside_weights.extend(weights)
        return {"token": token}

    def load_other(same, other):
        arrays = [kept["w0"], kept["w1"], kept["w2"]]
        arrays, same[1][1] = barrier((arrays, same[1][1]))
        weights, token = fetch(arrays)
        beside_weights.extend(weights)
        kept["token2"] = token
        p0, p1 = serve(0, 1, same[:2])
        return {("p", 0): p0, ("p", 1): p1}

    def serve(first, count, blocks):
        halves = [h for block in blocks for h in block]
        weights = beside_weights + [kept["token"], kept["token2"]]
        outs = experts(slots, first, count, gain, *kept["tables"], halves, weights)
        return [outs[i : i + 2] for i in range(0, len(outs), 2)]

    def serve_same(r):
        def step(same, other):
            p0, p1 = serve(r, 1, same[r : r + 2])
            return {("p", r): p0, ("p", r + 1): p1}

        return step

    def serve_other(r):
        def step(same, other):
            q0, q1 = serve(r + 1, 1, other[r : r + 2])
            return {("q", r): q0, ("q", r + 1): q1}

        return step

    def serve_two(same, other):
        p, q = serve(ring - 2, 1, [same[ring - 2], other[ring - 2]])
        return {("p", ring - 2): p, ("q", ring - 2): q}

    beside = [load_mine, load_other, serve_other(0)]
    for r in range(2, ring - 2, 2):
        beside += [serve_same(r), serve_other(r)]
    beside.append(serve_two)
    x_same, x_other = gather_halves([x_near, x_far], beside, [x_near_later, x_far])
    p = [kept["p", r] for r in range(ring - 1)]
    q = [kept["q", r] for r in range(ring - 1)]
    for parts, part in zip((p, q), serve(ring - 1, 1, [x_same[-1], x_other[-1]])):
        parts.append(part)

    def add(*terms):
        return sum(t.astype(jnp.float32) for t in terms).astype(jnp.bfloat16)

    extra = send_forward(q[1][1])
    came = [None, None]
    own_q = list(q[0])
    for r in range(1, ring):
        crossed = [send_across(q[r][0]), None]
        if r == 2:
            crossed[1] = send_across(add(q[r][1], extra))
        elif r > 2:
            crossed[1] = send_across(q[r][1])
        second = p[r][1]
        for h in range(2):
            terms = [(p[r][0], second)[h], came[h], crossed[h]]
            terms = [t for t in terms if t is not None]
            total = add(*terms) if len(terms) > 1 else terms[0]
            if h == 0:
                total, second = barrier((total, second))
            if r == ring - 2:
                total, own_q[h] = barrier((total, own_q[h]))
            came[h] = send_forward(total)
    crossed = [send_across(h) for h in own_q]
    mixed = [mixed_near, mixed_far]
    return finish(*[[mixed[h], p[0][h], came[h], crossed[h]] for h in range(2)])


def solution(mesh):
    placed = (
        P(("groups", "wide"), None),
        P(("groups", "wide"), None),
        P(("groups", "wide"), None),
        P(("groups", "wide"), None),
        P(("groups", "wide"), None, None),
        P(("groups", "wide"), None, None),
        P("groups"),
        P("wide", None),
        P(),
        P(("groups", "wide"), None),
        P(("groups", "wide"), None),
        P("wide", None, None),
        P("wide", None, None),
        P("wide", None, None),
    )
    return jax.shard_map(
        per_device,
        mesh=mesh,
        in_specs=placed,
        out_specs=P(("groups", "wide"), None),
        check_vma=False,
    )
```

```python
import functools

import jax
import jax.numpy as jnp
from jax import lax
from jax.experimental import pallas as pl
from jax.experimental.pallas import tpu as pltpu
from jax.sharding import PartitionSpec as P

HEAD = 128
KEY_BLOCK = 1024
LOG2E = 1.4426950408889634
NEG = -1e30
MIB = 1 << 20

VMEM = pl.BlockSpec(memory_space=pltpu.VMEM)
SMEM = pl.BlockSpec(memory_space=pltpu.SMEM)
ANY = pl.BlockSpec(memory_space=pl.ANY)


def place_of(ring):
    me = lax.axis_index("wide")
    return me // 4 % ring, me // 2 % 2, me % 2


def dot(a, b):
    return jnp.dot(a, b, preferred_element_type=jnp.float32)


def attention_kernel(
    part, len_ref, q_ref, nk_ref, nv_ref, k_any, v_any, o_ref, q_all, scores, top, acc, total, k_ref, v_ref, sems
):
    tokens = q_ref.shape[0]
    heads = q_ref.shape[1] // HEAD
    cache = k_any.shape[0]
    length = len_ref[lax.axis_index("wide")]
    blocks = (length + KEY_BLOCK - 1) // KEY_BLOCK
    scale = jnp.float32(HEAD**-0.5 * LOG2E)
    at = pl.ds(part * HEAD, HEAD)
    copies = [
        pltpu.make_async_copy(any_ref.at[:, at], ref, sems.at[i])
        for i, (any_ref, ref) in enumerate(((k_any, k_ref), (v_any, v_ref)))
    ]
    for copy in copies:
        copy.start()

    for h in range(heads):
        q_all[h * tokens : (h + 1) * tokens, :] = q_ref[:, h * HEAD : (h + 1) * HEAD]

    def scores_of(k):
        return lax.dot_general(
            q_all[...], k, (((1,), (1,)), ((), ())), preferred_element_type=jnp.float32
        )

    def fold(x, op):
        parts = [x[:, i : i + HEAD] for i in range(0, x.shape[1], HEAD)]
        while len(parts) > 1:
            parts = [op(*parts[i : i + 2]) if i + 1 < len(parts) else parts[i] for i in range(0, len(parts), 2)]
        return parts[0]

    s = scores_of(nk_ref[...])
    row = lax.broadcasted_iota(jnp.int32, s.shape, 0) % tokens
    col = lax.broadcasted_iota(jnp.int32, s.shape, 1)
    s = jnp.where(col <= row, s, NEG)
    scores[:, cache:] = s
    top[...] = fold(s, jnp.maximum)

    def score(i, carry):
        at = pl.ds(pl.multiple_of(i * KEY_BLOCK, KEY_BLOCK), KEY_BLOCK)
        s = scores_of(k_ref[at, :])
        pos = lax.broadcasted_iota(jnp.int32, s.shape, 1)
        s = jnp.where(pos < length - i * KEY_BLOCK, s, NEG)
        scores[:, at] = s
        top[...] = jnp.maximum(top[...], fold(s, jnp.maximum))
        return carry

    copies[0].wait()
    lax.fori_loop(0, blocks, score, 0)
    best = jnp.max(top[...], axis=1, keepdims=True) * scale
    top[...] = jnp.broadcast_to(best, top.shape)

    def weigh(s):
        shift = jnp.concatenate([top[...]] * (s.shape[1] // HEAD), axis=1)
        return jnp.exp2(s * scale - shift)

    w = weigh(scores[:, cache:])
    total[...] = fold(w, jnp.add)
    acc[...] = dot(w.astype(jnp.bfloat16), nv_ref[...])

    def add_block(i, carry):
        at = pl.ds(pl.multiple_of(i * KEY_BLOCK, KEY_BLOCK), KEY_BLOCK)
        w = weigh(scores[:, at])
        total[...] += fold(w, jnp.add)
        acc[...] += dot(w.astype(jnp.bfloat16), v_ref[at, :])
        return carry

    copies[1].wait()
    lax.fori_loop(0, blocks, add_block, 0)
    out = (acc[...] / jnp.sum(total[...], axis=1, keepdims=True)).astype(jnp.bfloat16)
    for h in range(heads):
        o_ref[:, h * HEAD : (h + 1) * HEAD] = out[h * tokens : (h + 1) * tokens, :]


def attention(part, parts, length, queries, new_keys, new_values, keys, values):
    tokens, width = queries.shape
    kv_heads = new_keys.shape[1] // HEAD
    g = part * kv_heads // parts
    group = width // parts
    cache = keys.shape[0]
    rows = group // HEAD * tokens
    keys, values = [pltpu.with_memory_space_constraint(a, pltpu.HBM) for a in (keys, values)]
    return pl.pallas_call(
        functools.partial(attention_kernel, g),
        grid=(1,),
        in_specs=[
            SMEM,
            pl.BlockSpec((tokens, group), lambda i: (0, part)),
            pl.BlockSpec((tokens, HEAD), lambda i: (0, g)),
            pl.BlockSpec((tokens, HEAD), lambda i: (0, g)),
            ANY,
            ANY,
        ],
        out_specs=pl.BlockSpec((tokens, group), lambda i: (0, 0)),
        out_shape=jax.ShapeDtypeStruct((tokens, group), jnp.bfloat16),
        scratch_shapes=[
            pltpu.VMEM((rows, HEAD), jnp.bfloat16),
            pltpu.VMEM((rows, cache + tokens), jnp.float32),
            pltpu.VMEM((rows, HEAD), jnp.float32),
            pltpu.VMEM((rows, HEAD), jnp.float32),
            pltpu.VMEM((rows, HEAD), jnp.float32),
            pltpu.VMEM((cache, HEAD), jnp.bfloat16),
            pltpu.VMEM((cache, HEAD), jnp.bfloat16),
            pltpu.SemaphoreType.DMA((2,)),
        ],
        compiler_params=pltpu.CompilerParams(vmem_limit_bytes=58 * MIB),
        cost_estimate=pl.CostEstimate(
            flops=20 * tokens * group * cache,
            bytes_accessed=4 * cache * HEAD,
            transcendentals=tokens * group // HEAD * cache,
        ),
        name="attention",
    )(length, queries, new_keys, new_values, keys, values)


def projection_kernel(n_pieces, n_blocks, *refs):
    pieces, w_refs = refs[:n_pieces], refs[n_pieces : n_pieces + n_blocks - 1]
    sum_out, left_out, left, weight, sems = refs[n_pieces + n_blocks - 1 :]
    tokens, group = pieces[0].shape
    rows = weight.shape[0] // n_blocks // 2
    each = left.shape[1] // group
    ring = n_blocks // 2
    place, row, core = place_of(ring)
    copies = []

    def first_row(b, part):
        z = lax.rem(place + ring - b % ring, ring)
        y = row if b < ring else 1 - row
        c = core if part == 0 else 1 - core
        return pl.multiple_of(((z * 2 + y) * 2 + c) * rows, rows)

    def begin(src, dst):
        copies.append(pltpu.make_async_copy(src, dst, sems.at[len(copies)]))
        copies[-1].start()

    for b in range(n_blocks - 1):
        for part in range(2):
            at = first_row(b, part)
            begin(w_refs[b].at[pl.ds(part * rows, rows)], weight.at[pl.ds(at, rows)])
    for i, piece in enumerate(pieces):
        dst = left.at[pl.ds(i // each * tokens, tokens), pl.ds(i % each * group, group)]
        begin(piece, dst)
    for part in range(2):
        at = first_row(n_blocks - 1, part)
        weight[pl.ds(at, rows), :] = jnp.zeros((rows, weight.shape[1]), weight.dtype)
    for copy in copies:
        copy.wait()
    sum_out[...] = dot(left[...], weight[...])
    if left_out.shape == left.shape:
        left_out[...] = left[...]
    else:
        for part in range(2):
            at = first_row(n_blocks - 1, part)
            left_out[:, part * rows : (part + 1) * rows] = left[:, pl.ds(at, rows)]


def projection(rows, pieces, count, blocks):
    tokens, group = pieces[0].shape
    width = len(pieces) // count * group
    n_blocks = len(blocks) + 1
    cols = blocks[0].shape[1]
    whole_tiles = rows % HEAD == 0
    pieces, blocks = [
        [pltpu.with_memory_space_constraint(a, pltpu.HBM) for a in arrays] for arrays in (pieces, blocks)
    ]
    total, left = pl.pallas_call(
        functools.partial(projection_kernel, len(pieces), n_blocks),
        in_specs=[ANY] * (len(pieces) + len(blocks)),
        out_specs=[VMEM] * 2,
        out_shape=[
            jax.ShapeDtypeStruct((count * tokens, cols), jnp.float32),
            jax.ShapeDtypeStruct((count * tokens, 2 * rows), jnp.bfloat16)
            if whole_tiles
            else jax.ShapeDtypeStruct((count * tokens, width), jnp.bfloat16),
        ],
        scratch_shapes=[
            pltpu.VMEM((count * tokens, width), jnp.bfloat16),
            pltpu.VMEM((width, cols), jnp.bfloat16),
            pltpu.SemaphoreType.DMA((2 * n_blocks - 2 + len(pieces),)),
        ],
        compiler_params=pltpu.CompilerParams(vmem_limit_bytes=20 * MIB),
        cost_estimate=pl.CostEstimate(
            flops=8 * tokens * width * cols, bytes_accessed=2 * width * cols, transcendentals=0
        ),
        name="projection",
    )(*pieces, *blocks)
    if not whole_tiles:
        ring = n_blocks // 2
        place, row, core = place_of(ring)
        source = ((place + 1) % ring * 2 + 1 - row) * 2
        parts = [
            lax.dynamic_slice_in_dim(left, (source + c) * rows, rows, 1) for c in (core, 1 - core)
        ]
        left = jnp.concatenate(parts, axis=1)
    return total, left


def complete_kernel(sum_ref, left_ref, first_ref, second_ref, *outs):
    tokens = outs[0].shape[0]
    half, rows = first_ref.shape[1], left_ref.shape[1]
    for h, w_ref in enumerate((first_ref, second_ref)):
        cols = slice(h * half, (h + 1) * half)
        whole = sum_ref[:, cols] + dot(left_ref[...], w_ref[:rows, :])
        for i, out in enumerate(outs):
            out[:, cols] = whole[i * tokens : (i + 1) * tokens].astype(out.dtype)


def complete(total, left, last, types):
    tokens = left.shape[0] // len(types)
    return pl.pallas_call(
        complete_kernel,
        in_specs=[VMEM] * 4,
        out_specs=[VMEM] * len(types),
        out_shape=[jax.ShapeDtypeStruct((tokens, total.shape[1]), t) for t in types],
        compiler_params=pltpu.CompilerParams(vmem_limit_bytes=16 * MIB),
        name="complete",
    )(total, left, *last)


def mix_kernel(far, residual_ref, gain_ref, *refs):
    parts, (mixed_ref, sent_ref) = refs[:-2], refs[-2:]
    cols = parts[0].shape[1]
    for i, part in enumerate(parts):
        core = lax.axis_index("wide") % 2
        side = lax.axis_index("groups") % 2
        at = (1 - core if i else core) * cols
        base = (1 - side if far else side) * 2 * cols
        here = pl.ds(pl.multiple_of(at, cols), cols)
        there = pl.ds(pl.multiple_of(base + at, cols), cols)
        mixed = residual_ref[:, there].astype(jnp.float32) + part[...].astype(jnp.float32)
        mixed_ref[:, here] = mixed
        sent_ref[:, here] = (mixed * gain_ref[:, there]).astype(jnp.bfloat16)


def mix(far, residual, gain, parts):
    shape = (residual.shape[0], residual.shape[1] // 2)
    residual = pltpu.with_memory_space_constraint(residual, pltpu.HBM)
    return pl.pallas_call(
        functools.partial(mix_kernel, far),
        in_specs=[VMEM] * (2 + len(parts)),
        out_specs=[VMEM] * 2,
        out_shape=[
            jax.ShapeDtypeStruct(shape, jnp.float32),
            jax.ShapeDtypeStruct(shape, jnp.bfloat16),
        ],
        compiler_params=pltpu.CompilerParams(vmem_limit_bytes=24 * MIB),
        cost_estimate=pl.CostEstimate(flops=0, bytes_accessed=0, transcendentals=0),
        name="mix",
    )(residual, gain, *parts)


def finish_kernel(*refs):
    out_ref = refs[-1]
    terms = (len(refs) - 1) // 2
    half = refs[0].shape[1]
    side = lax.axis_index("groups") % 2
    for h in range(2):
        total = refs[h * terms][...]
        for ref in refs[h * terms + 1 : (h + 1) * terms]:
            total = total + ref[...].astype(jnp.float32)
        at = side if h == 0 else 1 - side
        out_ref[:, pl.ds(pl.multiple_of(at * half, half), half)] = total.astype(out_ref.dtype)


def finish(first, second):
    tokens, half = first[0].shape
    rows = max(16, tokens // 4)
    part = pl.BlockSpec((rows, half), lambda i: (i, 0))
    return pl.pallas_call(
        finish_kernel,
        grid=(tokens // rows,),
        in_specs=[part] * (len(first) + len(second)),
        out_specs=pl.BlockSpec((rows, 2 * half), lambda i: (i, 0)),
        out_shape=jax.ShapeDtypeStruct((tokens, 2 * half), jnp.bfloat16),
        compiler_params=pltpu.CompilerParams(vmem_limit_bytes=24 * MIB),
        name="finish",
    )(*first, *second)


def routing_kernel(cap, n_blocks, *refs):
    sources, refs = refs[: n_blocks + 1], refs[n_blocks + 1 :]
    rows_ref, cols_ref, shares_ref, table_ref, mask, sems = refs
    tokens = mask.shape[1]
    top, lines, width = 8, table_ref.shape[1], table_ref.shape[2]
    copies = []
    for b, source in enumerate(sources):
        src = source.at[pl.ds(source.shape[0] - lines, lines)]
        if b < n_blocks - 1:
            dst = table_ref.at[b]
        else:
            at = (b - n_blocks + 1) * (width // 2)
            dst = table_ref.at[n_blocks - 1, :, pl.ds(at, width // 2)]
        copies.append(pltpu.make_async_copy(src, dst, sems.at[b]))
        copies[-1].start()
    for copy in copies:
        copy.wait()
    me = lax.axis_index("wide")
    served = [me.astype(jnp.float32), (me + 1 - 2 * (me % 2)).astype(jnp.float32)]
    for b in range(n_blocks):
        parts = [
            table_ref[b, :, i * tokens : (i + 1) * tokens].astype(jnp.float32)[:top]
            for i in range(3)
        ]
        ids, score = parts[0], parts[1] + parts[2]
        share = score / jnp.sum(score, axis=0, keepdims=True)
        at = slice(b % 2 * tokens, (b % 2 + 1) * tokens)
        for e in range(2):
            hit = ids == served[e]
            mask[2 * b + e : 2 * b + e + 1, :] = jnp.max(
                jnp.where(hit, 1.0, 0.0), axis=0, keepdims=True
            )
            shares_ref[b // 2, e : e + 1, at] = jnp.sum(
                jnp.where(hit, share, 0.0), axis=0, keepdims=True
            )
    first = lax.broadcasted_iota(jnp.int32, (tokens, tokens), 0)
    second = lax.broadcasted_iota(jnp.int32, (tokens, tokens), 1)
    before = jnp.where(first < second, 1.0, 0.0).astype(jnp.bfloat16)
    same = jnp.where(first == second, 1.0, 0.0).astype(jnp.bfloat16)
    there = mask[...]
    rank = dot(there.astype(jnp.bfloat16), before)
    line = lax.broadcasted_iota(jnp.int32, rank.shape, 0)
    slot = jnp.where(there > 0.5, rank + jnp.where(line // 2 % 2 == 1, float(cap), 0.0), -512.0)
    columns = lax.dot_general(
        same, slot.astype(jnp.bfloat16), (((1,), (1,)), ((), ())), preferred_element_type=jnp.float32
    )
    for b in range(n_blocks):
        at = slice(b % 2 * tokens, (b % 2 + 1) * tokens)
        pair = slice(2 * b, 2 * b + 2)
        rows_ref[b // 2, :, at] = slot[pair].astype(jnp.int32)
        cols_ref[b // 2, at, :] = columns[:, pair].astype(jnp.int32)


def routing(cap, tokens, lines, blocks):
    blocks = [pltpu.with_memory_space_constraint(b, pltpu.HBM) for b in blocks]
    n_blocks = len(blocks) - 1
    pairs = n_blocks // 2
    rows = jax.ShapeDtypeStruct((pairs, 2, 2 * tokens), jnp.int32)
    return pl.pallas_call(
        functools.partial(routing_kernel, cap, n_blocks),
        in_specs=[ANY] * len(blocks),
        out_specs=[VMEM] * 3,
        out_shape=[
            rows,
            jax.ShapeDtypeStruct((pairs, 2 * tokens, 2), jnp.int32),
            jax.ShapeDtypeStruct(rows.shape, jnp.float32),
        ],
        scratch_shapes=[
            pltpu.VMEM((n_blocks, lines, blocks[0].shape[1]), jnp.bfloat16),
            pltpu.VMEM((2 * n_blocks, tokens), jnp.float32),
            pltpu.SemaphoreType.DMA((n_blocks + 1,)),
        ],
        compiler_params=pltpu.CompilerParams(vmem_limit_bytes=16 * MIB),
        cost_estimate=pl.CostEstimate(flops=0, bytes_accessed=0, transcendentals=0),
        name="routing",
    )(*blocks)


def fetch_kernel(*refs):
    count = (len(refs) - 2) // 2
    token, sems = refs[-2:]
    token[...] = jnp.zeros_like(token)
    copies = [
        pltpu.make_async_copy(refs[i], refs[count + i], sems.at[i]) for i in range(count)
    ]
    for copy in copies:
        copy.start()
    for copy in copies:
        copy.wait()


def fetch(arrays):
    arrays = [pltpu.with_memory_space_constraint(a, pltpu.HBM) for a in arrays]
    *there, token = pl.pallas_call(
        fetch_kernel,
        in_specs=[ANY] * len(arrays),
        out_specs=[VMEM] * (len(arrays) + 1),
        out_shape=[pltpu.VMEM(a.shape, a.dtype) for a in arrays]
        + [jax.ShapeDtypeStruct((8, HEAD), jnp.float32)],
        scratch_shapes=[pltpu.SemaphoreType.DMA((len(arrays),))],
        compiler_params=pltpu.CompilerParams(vmem_limit_bytes=24 * MIB),
        cost_estimate=pl.CostEstimate(flops=0, bytes_accessed=0, transcendentals=0),
        name="fetch",
    )(*arrays)
    return there, token


def experts_kernel(first_pair, pairs, n_in, n_out, slots, gain_ref, slot_rows, slot_cols, share_rows, *refs):
    x_refs = refs[:n_in]
    w_refs = refs[n_in : n_in + 6]
    out_refs = refs[n_in + 8 : n_in + 8 + n_out]
    xs, rows_in, act, scaled, x_sem = refs[n_in + 8 + n_out :]
    depth = xs.shape[1]
    pair_tokens = xs.shape[0] // pairs
    block = pair_tokens // 2
    hidden = act.shape[1]

    half = depth // 2
    side = lax.axis_index("groups") % 2
    starts = [pl.multiple_of(side * half, half), pl.multiple_of((1 - side) * half, half)]
    x_copies = []
    for i in range(n_in):
        dst = xs.at[pl.ds(i // 2 * block, block), pl.ds(starts[i % 2], half)]
        x_copies.append(pltpu.make_async_copy(x_refs[i], dst, x_sem.at[i]))
        x_copies[-1].start()
    for copy in x_copies:
        copy.wait()

    shares = []
    for p in range(pairs):
        row = lax.broadcasted_iota(jnp.int32, (2 * slots, pair_tokens), 0)
        first = row == slot_rows[first_pair + p, 0:1, :]
        second = row - slots == slot_rows[first_pair + p, 1:2, :]
        pick = jnp.where(first | second, 1.0, 0.0).astype(jnp.bfloat16)
        weight = jnp.where(first, share_rows[first_pair + p, 0:1, :], 0.0) + jnp.where(
            second, share_rows[first_pair + p, 1:2, :], 0.0
        )
        shares.append(jnp.sum(weight, axis=1, keepdims=True))
        step = min(1024, depth)
        for c in range(0, depth, step):
            got = dot(pick, xs[p * pair_tokens : (p + 1) * pair_tokens, c : c + step])
            got = got.astype(jnp.bfloat16)
            rows_in[0, p * slots : (p + 1) * slots, c : c + step] = got[:slots]
            rows_in[1, p * slots : (p + 1) * slots, c : c + step] = got[slots:]

    inverse = 1.0 / gain_ref[...]
    for e in range(2):
        x = rows_in[e]
        squares = 0.0
        for c in range(0, depth, HEAD):
            part = x[:, c : c + HEAD].astype(jnp.float32) * inverse[:, c : c + HEAD]
            squares = squares + part * part
        factor = lax.rsqrt(jnp.sum(squares, axis=1, keepdims=True) / depth + 1e-06)
        gate = dot(x, w_refs[3 * e][...]) * factor
        up = dot(x, w_refs[3 * e + 1][...]) * factor
        act[...] = (gate / (1.0 + jnp.exp(-gate)) * up).astype(jnp.bfloat16)
        share = jnp.concatenate([s[e * slots : (e + 1) * slots] for s in shares], axis=0)
        y = (dot(act[...], w_refs[3 * e + 2][...]) * share).astype(jnp.bfloat16)
        for p in range(pairs):
            scaled[p, e * slots : (e + 1) * slots, :] = y[p * slots : (p + 1) * slots]

    for p in range(pairs):
        lane = lax.broadcasted_iota(jnp.int32, (pair_tokens, 2 * slots), 1)
        back = lane == slot_cols[first_pair + p, :, 0:1]
        back = back | (lane - slots == slot_cols[first_pair + p, :, 1:2])
        back = jnp.where(back, 1.0, 0.0).astype(jnp.bfloat16)
        for h in range(2):
            got = dot(back, scaled[p, :, pl.ds(starts[h], half)]).astype(jnp.bfloat16)
            for b in range(2):
                out_refs[4 * p + 2 * b + h][...] = got[b * block : (b + 1) * block]


def experts(slots, first_pair, pairs, gain, slot_rows, slot_cols, share_rows, x_parts, weights):
    pair_tokens = slot_rows.shape[2]
    block = pair_tokens // 2
    depth, hidden = weights[0].shape
    n_in = n_out = len(x_parts)
    return pl.pallas_call(
        functools.partial(experts_kernel, first_pair, pairs, n_in, n_out, slots),
        in_specs=[VMEM] * 4 + [ANY] * n_in + [VMEM] * 6 + [ANY] * 2,
        out_specs=[VMEM] * n_out,
        out_shape=[jax.ShapeDtypeStruct((block, depth // 2), jnp.bfloat16)] * n_out,
        scratch_shapes=[
            pltpu.VMEM((pairs * pair_tokens, depth), jnp.bfloat16),
            pltpu.VMEM((2, pairs * slots, depth), jnp.bfloat16),
            pltpu.VMEM((pairs * slots, hidden), jnp.bfloat16),
            pltpu.VMEM((pairs, 2 * slots, depth), jnp.bfloat16),
            pltpu.SemaphoreType.DMA((n_in,)),
        ],
        compiler_params=pltpu.CompilerParams(vmem_limit_bytes=22 * MIB),
        cost_estimate=pl.CostEstimate(
            flops=12 * pairs * slots * depth * hidden,
            bytes_accessed=12 * depth * hidden,
            transcendentals=0,
        ),
        name="experts",
    )(gain, slot_rows, slot_cols, share_rows, *x_parts, *weights)


def permutations(devices):
    cores, rows = 2, 2
    ring = devices // (cores * rows)

    def index(z, y, c):
        return (z % ring * rows + y % rows) * cores + c % cores

    def shift(dz, dy=0, dc=0):
        return [
            (index(z, y, c), index(z + dz + ring, y + dy, c + dc))
            for z in range(ring)
            for y in range(rows)
            for c in range(cores)
        ]

    return ring, shift


def per_device(
    residual,
    queries,
    new_keys,
    new_values,
    cache_keys,
    cache_values,
    cache_len,
    o_weight,
    norm_gain,
    expert_ids,
    gate_raw,
    w_gate,
    w_up,
    w_down,
):
    devices = lax.axis_size("wide")
    replicas = lax.axis_size("groups")
    me = lax.axis_index("wide")
    tokens, depth = residual.shape
    top = expert_ids.shape[1]
    half = depth // 2
    ring, shift = permutations(devices)
    core = me % 2
    side = lax.axis_index("groups") % 2

    def sender(*by):
        return lambda x: lax.ppermute(x, "wide", shift(*by))

    def side_sender(*by):
        pairs = [
            (g * devices + a, (g ^ 1) * devices + b)
            for g in range(replicas)
            for a, b in shift(*by)
        ]
        return lambda x: lax.ppermute(x, ("groups", "wide"), pairs)

    send_forward, send_backward = sender(1), sender(-1)
    send_across, send_core = sender(0, 1), sender(0, 0, 1)
    send_side, send_corner = side_sender(0), side_sender(0, 0, 1)
    barrier = lax.optimization_barrier

    def gather_whole(own, beside):
        same, other = [own], []
        for r in range(1, ring):
            moved, crossed = send_forward(same[-1]), send_across(same[-1])
            new = beside[r - 1](same, other) if r <= len(beside) else {}
            moved, crossed, new = barrier((moved, crossed, new))
            kept.update(new)
            same.append(moved)
            other.append(crossed)
        cut = own.shape[1] // 2
        last = [send_across(same[-1][:, :cut]), send_forward(other[-1][:, cut:])]
        for step in beside[ring - 1 :]:
            last, new = barrier((last, step(same, other)))
            kept.update(new)
        return same, other, last

    def gather_halves(own, beside, held):
        same, other = [list(own)], []
        for r in range(1, ring):
            moved = [send_forward(h) for h in same[-1]]
            crossed = [send_across(h) for h in same[-1]]
            if r == 1:
                same[0] = list(held)
            new = beside[r - 1](same, other) if r <= len(beside) else {}
            moved[0], crossed[0] = barrier((moved[0], crossed[0]))
            moved[1], crossed[1], new = barrier((moved[1], crossed[1], new))
            kept.update(new)
            same.append(moved)
            other.append(crossed)
        last = [send_forward(other[-1][0]), send_across(same[-1][1])]
        for step in beside[ring - 1 :]:
            last, new = barrier((last, step(same, other)))
            kept.update(new)
        other.append(last)
        return same, other

    kept = {}

    def nothing(same, other):
        return {}

    cols = depth // 4
    quarter = 2 * side + core
    keep = lax.dynamic_slice_in_dim(o_weight, quarter * cols, cols, 1)
    give = lax.dynamic_slice_in_dim(o_weight, (quarter ^ 1) * cols, cols, 1)
    high = gate_raw.astype(jnp.bfloat16)
    low = (gate_raw - high.astype(jnp.float32)).astype(jnp.bfloat16)
    table = jnp.concatenate([expert_ids.astype(jnp.bfloat16).T, high.T, low.T], axis=1)
    lines = 16
    table = jnp.pad(table, ((0, lines - top), (0, cols - 3 * tokens)))
    own_block = jnp.concatenate([keep, send_core(give), table], axis=0)
    length = cache_len
    mine = [w_gate[0], w_up[0], w_down[0]]
    length, own_block, mine = barrier((length, own_block, mine))
    operands = (queries, new_keys, new_values, cache_keys[0], cache_values[0])

    late = {}
    beside_weights = []

    def attend_first(same, other):
        return {"a0": attention(0, 2, length, *operands), "w0": send_core(mine[0])}

    def attend_second(same, other):
        begin, kept["a0"] = barrier((length, kept["a0"]))
        return {
            "a1": attention(1, 2, begin, *operands),
            "side0": send_side(kept["a0"]),
            "w1": send_core(mine[1]),
        }

    def swap_first(same, other):
        late["side1"] = send_side(kept["a1"])
        return {"core0": send_core(kept["a0"]), "w2": send_core(mine[2])}

    def project(same, other):
        kept["core1"] = send_core(kept["a1"])
        kept["corner0"] = send_core(kept["side0"])
        kept["corner1"] = send_core(late["side1"])
        kept.update(late)
        pieces = [kept[name + str(g)] for name in ("a", "core", "side", "corner") for g in range(2)]
        return {"sum": projection(o_weight.shape[0], pieces, 4, same + other)}

    w_same, w_other, w_last = gather_whole(
        own_block, [attend_first, attend_second, swap_first] + [nothing] * (ring - 4) + [project]
    )
    types = [jnp.float32, jnp.float32, jnp.bfloat16, jnp.bfloat16]
    own_part, core_part, side_part, corner_part = complete(
        *kept["sum"], w_last, types
    )

    gain = norm_gain.reshape(1, -1)
    near = [own_part, send_core(core_part)]
    far = [send_side(side_part), send_corner(corner_part)]
    mixed_near, x_near = mix(False, residual, gain, near)
    cap = tokens * top // devices + max(2, tokens * top // (8 * devices))
    slots = -(-2 * cap // 16) * 16
    w_blocks, x_near_later = barrier((w_same + w_other + w_last, x_near))
    order = []
    for r in range(0, ring - 2, 2):
        order += w_blocks[r : r + 2] + w_blocks[ring + r : ring + r + 2]
    order += [w_blocks[ring - 2], w_blocks[-3], w_blocks[ring - 1]] + w_blocks[-2:]
    tables = routing(cap, tokens, lines, order)
    far, tables = barrier((far, tables))
    mixed_far, x_far = mix(True, residual, gain, far)

    def load_mine(same, other):
        arrays, kept["tables"], same[0][1] = barrier((mine, tables, same[0][1]))
        weights, token = fetch(arrays)
        beside_weights.extend(weights)
        return {"token": token}

    def load_other(same, other):
        arrays = [kept["w0"], kept["w1"], kept["w2"]]
        arrays, same[1][1] = barrier((arrays, same[1][1]))
        weights, token = fetch(arrays)
        beside_weights.extend(weights)
        kept["token2"] = token
        p0, p1 = serve(0, 1, same[:2])
        kept["p", 0], kept["p", 1] = p0, p1
        return {}

    def serve(first, count, blocks):
        halves = [h for block in blocks for h in block]
        weights = beside_weights + [kept["token"], kept["token2"]]
        outs = experts(slots, first, count, gain, *kept["tables"], halves, weights)
        return [outs[i : i + 2] for i in range(0, len(outs), 2)]

    def serve_same(r):
        def step(same, other):
            p0, p1 = serve(r, 1, same[r : r + 2])
            return {("p", r): p0, ("p", r + 1): p1}

        return step

    def serve_other(r):
        def step(same, other):
            kept["q", r], kept["q", r + 1] = serve(r + 1, 1, other[r : r + 2])
            return {}

        return step

    def serve_two(same, other):
        p, q = serve(ring - 2, 1, [same[ring - 2], other[ring - 2]])
        kept["p", ring - 2], kept["q", ring - 2] = p, q
        return {}

    beside = [load_mine, load_other, serve_other(0)]
    for r in range(2, ring - 2, 2):
        beside += [serve_same(r), serve_other(r)]
    beside.append(serve_two)
    x_same, x_other = gather_halves([x_near, x_far], beside, [x_near_later, x_far])
    p = [kept["p", r] for r in range(ring - 1)]
    q = [kept["q", r] for r in range(ring - 1)]
    for parts, part in zip((p, q), serve(ring - 1, 1, [x_same[-1], x_other[-1]])):
        parts.append(part)

    def add(*terms):
        return sum(t.astype(jnp.float32) for t in terms).astype(jnp.bfloat16)

    extra = send_forward(q[1][1])
    came = [None, None]
    own_q = list(q[0])
    for r in range(1, ring):
        crossed = [send_across(q[r][0]), None]
        if r == 2:
            crossed[1] = send_across(add(q[r][1], extra))
        elif r > 2:
            crossed[1] = send_across(q[r][1])
        second = p[r][1]
        for h in range(2):
            terms = [(p[r][0], second)[h], came[h], crossed[h]]
            terms = [t for t in terms if t is not None]
            total = add(*terms) if len(terms) > 1 else terms[0]
            if h == 0:
                total, second = barrier((total, second))
            if r == ring - 2:
                total, own_q[h] = barrier((total, own_q[h]))
            came[h] = send_forward(total)
    crossed = [send_across(h) for h in own_q]
    mixed = [mixed_near, mixed_far]
    return finish(*[[mixed[h], p[0][h], came[h], crossed[h]] for h in range(2)])


def solution(mesh):
    placed = (
        P(("groups", "wide"), None),
        P(("groups", "wide"), None),
        P(("groups", "wide"), None),
        P(("groups", "wide"), None),
        P(("groups", "wide"), None, None),
        P(("groups", "wide"), None, None),
        P("groups"),
        P("wide", None),
        P(),
        P(("groups", "wide"), None),
        P(("groups", "wide"), None),
        P("wide", None, None),
        P("wide", None, None),
        P("wide", None, None),
    )
    return jax.shard_map(
        per_device,
        mesh=mesh,
        in_specs=placed,
        out_specs=P(("groups", "wide"), None),
        check_vma=False,
    )
```
